32 devices in a mesh: depth: 4 (over x, core), height: 4 (over z), filt: 2 (over y).
Axes of the slice: x: 2, y: 2, z: 4, core: 2. Of those that a mesh axis runs over, the one named last changes fastest.
Arguments:
- volume: bfloat16 [16, 16, 64, 256], P('depth', 'height', None, 'filt'), may hold values from -6 to 6
- kernel_one: bfloat16 [3, 3, 3, 256, 256], replicated, may hold values from -0.078125 to 0.078125
- bias_one: float32 [256], replicated, may hold values from -3 to 3
- kernel_two: bfloat16 [3, 3, 3, 256, 256], replicated, may hold values from -0.078125 to 0.078125
- bias_two: float32 [256], replicated, may hold values from -3 to 3
Outputs:
- features: bfloat16 [16, 16, 64, 256], P('depth', 'height', None, 'filt')
The draws below stay inside these ranges and needn't reach their ends.
All inputs are finite; a program needn't handle non-finite values.
Results may differ from the reference program's by a relative error of at most 0.0044.
Values may be sent and summed in bfloat16 or wider, within the bound.
No kernel may reach another device: no remote copies, remote signals or barrier semaphores. Data moves between devices by JAX's collectives and lax.ppermute only.
A program may use at most 64 MiB of HBM per device.

```python
import jax
import jax.numpy as jnp
from jax import lax

CHANNELS = 256
WID = 64
DEPTH_ALL = 16
HEIGHT_ALL = 16


def steps_of(key, shape, shards, smallest, largest):
    level, own = 1.0, jax.random.fold_in(key, 6)
    for dim, blocks in shards:
        draws = jnp.exp(jax.random.uniform(jax.random.fold_in(own, dim), (blocks,), jnp.float32, smallest / len(shards), largest / len(shards)))
        level = level * jnp.repeat(draws, shape[dim] // blocks).reshape([-1 if axis == dim else 1 for axis in range(len(shape))])
    return level


def centred(stream_key, shape, spread, most, split=(), dtype=jnp.bfloat16):
    array = jax.random.normal(stream_key, shape, jnp.float32) * spread
    if len(split) > 0:
        array = steps_of(stream_key, shape, split, -0.22, 0.18) * array
    return jnp.clip(array, min=-most, max=most).astype(dtype)


def setup_inputs(seed: int = 0) -> dict:
    streams_of = jax.random.split(jax.random.key(seed), 6)
    return {
        "volume": centred(streams_of[0], (DEPTH_ALL, HEIGHT_ALL, WID, CHANNELS), 1.0, 6.0, ((0, 4), (1, 4), (3, 2))),
        "kernel_one": centred(streams_of[1], (3, 3, 3, CHANNELS, CHANNELS), (27 * CHANNELS) ** -0.5, 0.078125),
        "bias_one": centred(streams_of[2], (CHANNELS,), 0.5, 3.0, (), jnp.float32),
        "kernel_two": centred(streams_of[3], (3, 3, 3, CHANNELS, CHANNELS), (27 * CHANNELS) ** -0.5, 0.078125),
        "bias_two": centred(streams_of[4], (CHANNELS,), 0.5, 3.0, (), jnp.float32),
    }


def leaky(value):
    return jnp.where(value > 0, value, 0.3 * value)


def convolve(field, kernel):
    out = lax.conv_general_dilated(field.astype(jnp.float32)[None], kernel.astype(jnp.float32), (1, 1, 1), [(1, 1), (1, 1), (1, 1)], dimension_numbers=("NDHWC", "DHWIO", "NDHWC"), precision=lax.Precision.HIGHEST)
    return out[0]


def reference(volume, kernel_one, bias_one, kernel_two, bias_two):
    hidden = leaky(convolve(volume, kernel_one) + bias_one).astype(jnp.bfloat16)
    return leaky(convolve(hidden, kernel_two) + bias_two).astype(jnp.bfloat16)
```

```python
import functools

import jax
import jax.numpy as jnp
from jax import lax
from jax.experimental import pallas as pl
from jax.experimental.pallas import tpu as pltpu
from jax.sharding import PartitionSpec as P


def leaky(value):
    return jnp.where(value > 0, value, 0.3 * value)


def exchange(first, last, axis):
    peers, index = lax.axis_size(axis), lax.axis_index(axis)
    odd = index % 2 == 1
    pairs = [(i, i + 1) for i in range(0, peers - 1, 2)]
    evens = [(i, i) for i in range(peers) if peers % 2 == 1 and i == peers - 1]
    gaps = [(i, i + 1) for i in range(1, peers - 1, 2)]
    rest = [(i, i) for i in range(peers) if i == 0 or (peers % 2 == 0 and i == peers - 1)]
    both = lambda p, own: p + [(j, i) for i, j in p] + own
    one = lax.ppermute(jnp.where(odd, first, last), axis, both(pairs, evens))
    two = lax.ppermute(jnp.where(odd, last, first), axis, both(gaps, rest))
    before = jnp.where(odd, one, two)
    after = jnp.where(odd, two, one)
    before = jnp.where(index == 0, jnp.zeros_like(before), before)
    after = jnp.where(index == peers - 1, jnp.zeros_like(after), after)
    return before, after


def to_columns(x, axis):
    peers, index = lax.axis_size(axis), lax.axis_index(axis)
    own = x.shape[2] // peers
    padded = jnp.pad(x, ((0, 0), (0, 0), (2, 2), (0, 0)))
    parts = [lax.dynamic_slice_in_dim(padded, index * own, own + 4, 2)]
    for s in range(1, peers):
        dest = (index + s) % peers
        part = lax.dynamic_slice_in_dim(padded, dest * own, own + 4, 2)
        parts.append(lax.ppermute(part, axis, [(i, (i + s) % peers) for i in range(peers)]))
    if peers == 2:
        return jnp.where(index == 0, jnp.concatenate(parts, 3), jnp.concatenate(parts[::-1], 3))
    stacked = jnp.stack(parts)
    order = (index - jnp.arange(peers)) % peers
    return jnp.concatenate([stacked[order[c]] for c in range(peers)], 3)


def to_channels(y, axis):
    peers, index = lax.axis_size(axis), lax.axis_index(axis)
    shard, own = y.shape[3] // peers, y.shape[2]
    parts = [lax.dynamic_slice_in_dim(y, index * shard, shard, 3)]
    for s in range(1, peers):
        dest = (index + s) % peers
        part = lax.dynamic_slice_in_dim(y, dest * shard, shard, 3)
        parts.append(lax.ppermute(part, axis, [(i, (i + s) % peers) for i in range(peers)]))
    if peers == 2:
        return jnp.where(index == 0, jnp.concatenate(parts, 2), jnp.concatenate(parts[::-1], 2))
    stacked = jnp.stack(parts)
    order = (index - jnp.arange(peers)) % peers
    return jnp.concatenate([stacked[order[c]] for c in range(peers)], 2)


def conv_kernel(sides, edges, xb, xc, xa, k1, b1, k2, b2, o_ref, x3, ef, e3, eb, h3):
    C = xc.shape[3]
    D, H, Wp = xc.shape[0], xc.shape[1], xc.shape[2]
    own = Wp - 4
    D2, H2, D1, H1, H0 = D + 4, H, D + 2, H - 2, H - 4
    index, peers = edges[4], edges[5]
    rows = [xb.at[d] for d in range(2)] + [xc.at[d] for d in range(D)] + [xa.at[d] for d in range(2)]
    for d in range(D2):
        x = rows[d][...]
        for c in range(3):
            x3[d, :, :, c * C:(c + 1) * C] = x[:, 1 + c:1 + c + own, :]
        for s in range(sides):
            low, high = x[:, 0:3, :], x[:, Wp - 3:Wp, :]
            if sides == 1:
                pick = jnp.where(index == 0, high, low)
            else:
                pick = low if s == 0 else high
            pick = pick.astype(jnp.float32)
            for l in range(0, C, 128):
                for h in range(H2):
                    ef[s, l // 128, pl.ds((d * H2 + h) * 8, 3), :] = pick[h, :, l:l + 128]
                for c in range(3):
                    e3[s, d, 0:H2, c * C + l:c * C + l + 128] = ef[s, l // 128, pl.ds(d * H2 * 8 + c, H2, stride=8), :]
            for b in range(3):
                eb[s, b, d] = e3[s, d, b:b + H2, :].astype(jnp.bfloat16)

    bias1 = b1[...]
    for d in range(0, D1, 2):
        main = 2 * H1 * own
        acc = jnp.zeros((main + sides * 2 * H2, C), jnp.float32)
        for a in range(3):
            for b in range(3):
                lhs = [x3[d + a:d + a + 2, b:b + H1].reshape(main, 3 * C)]
                lhs += [eb[s, b, d + a:d + a + 2].reshape(2 * H2, 3 * C) for s in range(sides)]
                acc += jnp.dot(jnp.concatenate(lhs, 0), k1[a, b].reshape(3 * C, C), preferred_element_type=jnp.float32)
        acc = leaky(acc + bias1)
        for q in range(2):
            hid = acc[q * H1 * own:(q + 1) * H1 * own].reshape(H1, own, C)
            ends = [acc[main + (s * 2 + q) * H2:main + (s * 2 + q + 1) * H2] for s in range(sides)]
            inside = True
            if d + q == 0:
                inside = edges[0] == 0
            if d + q == D1 - 1:
                inside = edges[1] == 0
            for h in range(H1):
                row = hid[h]
                ok = inside
                if h == 0:
                    ok = jnp.logical_and(ok, edges[2] == 0)
                if h == H1 - 1:
                    ok = jnp.logical_and(ok, edges[3] == 0)
                if ok is not True:
                    row = jnp.where(ok, row, 0.0)
                none = jnp.zeros((1, C), jnp.float32)
                if sides == 1:
                    end = ends[0][h:h + 1]
                    left = jnp.where(index == 0, none, end)
                    right = jnp.where(index == 0, end, none)
                else:
                    left = jnp.where(index == 0, none, ends[0][h:h + 1])
                    right = jnp.where(index == peers - 1, none, ends[1][h:h + 1])
                if ok is not True:
                    left, right = jnp.where(ok, left, 0.0), jnp.where(ok, right, 0.0)
                column = lax.broadcasted_iota(jnp.int32, (own, C), 0)
                h3[d + q, h, :, 0:C] = jnp.where(column == 0, left, pltpu.roll(row, 1, 0)).astype(jnp.bfloat16)
                h3[d + q, h, :, C:2 * C] = row.astype(jnp.bfloat16)
                h3[d + q, h, :, 2 * C:] = jnp.where(column == own - 1, right, pltpu.roll(row, own - 1, 0)).astype(jnp.bfloat16)

    bias2 = b2[...]
    for d in range(0, D, 2):
        acc = jnp.zeros((2 * H0 * own, C), jnp.float32)
        for a in range(3):
            for b in range(3):
                acc += jnp.dot(h3[d + a:d + a + 2, b:b + H0].reshape(2 * H0 * own, 3 * C), k2[a, b].reshape(3 * C, C), preferred_element_type=jnp.float32)
        o_ref[d:d + 2] = leaky(acc + bias2).astype(jnp.bfloat16).reshape(2, H0, own, C)


def convolutions(xb, xc, xa, k1, b1, k2, b2):
    D, H, Wp, C = xc.shape
    own = Wp - 4
    d, h, f = (lax.axis_index(a) for a in ("depth", "height", "filt"))
    nd, nh, nf = (lax.axis_size(a) for a in ("depth", "height", "filt"))
    edges = jnp.stack([d == 0, d == nd - 1, h == 0, h == nh - 1, f, jnp.int32(nf)]).astype(jnp.int32)
    sides = 1 if nf == 2 else 2
    vmem = pl.BlockSpec(memory_space=pltpu.VMEM)
    return pl.pallas_call(
        functools.partial(conv_kernel, sides),
        out_shape=jax.ShapeDtypeStruct((D, H - 4, own, C), jnp.bfloat16),
        in_specs=[pl.BlockSpec(memory_space=pltpu.SMEM)] + [vmem] * 7,
        out_specs=vmem,
        scratch_shapes=[
            pltpu.VMEM((D + 4, H, own, 3 * C), jnp.bfloat16),
            pltpu.VMEM((sides, C // 128, (D + 4) * H * 8, 128), jnp.float32),
            pltpu.VMEM((sides, D + 4, 2 * H, 3 * C), jnp.float32),
            pltpu.VMEM((sides, 3, D + 4, H, 3 * C), jnp.bfloat16),
            pltpu.VMEM((D + 2, H - 2, own, 3 * C), jnp.bfloat16),
        ],
        compiler_params=pltpu.CompilerParams(vmem_limit_bytes=40 * 2**20),
        cost_estimate=pl.CostEstimate(flops=2 * 27 * C * C * own * ((D + 2) * (H - 2) + D * (H - 4)), bytes_accessed=8 * 2**20, transcendentals=0),
    )(edges, xb, xc, xa, k1, b1, k2, b2)


def body(volume, kernel_one, bias_one, kernel_two, bias_two):
    whole = to_columns(volume, "filt")
    before, after = exchange(whole[:, :2], whole[:, -2:], "height")
    tall = jnp.concatenate([before, whole, after], 1)
    front, back = exchange(tall[:2], tall[-2:], "depth")
    out = convolutions(front, tall, back, kernel_one, bias_one.reshape(1, -1), kernel_two, bias_two.reshape(1, -1))
    return to_channels(out, "filt")


def solution(mesh):
    in_specs = (P("depth", "height", None, "filt"), P(), P(), P(), P())
    out_specs = P("depth", "height", None, "filt")
    return jax.shard_map(body, mesh=mesh, in_specs=in_specs, out_specs=out_specs, check_vma=False)
```

```python
import functools

import jax
import jax.numpy as jnp
from jax import lax
from jax.experimental import pallas as pl
from jax.experimental.pallas import tpu as pltpu
from jax.sharding import PartitionSpec as P

VMEM = pl.BlockSpec(memory_space=pltpu.VMEM)
SMEM = pl.BlockSpec(memory_space=pltpu.SMEM)
ANY = pl.BlockSpec(memory_space=pl.ANY)


def leaky(value):
    return jnp.where(value > 0, value, 0.3 * value)


def pairings(peers):
    rounds = []
    for start in (0, 1):
        pairs = [(i, i + 1) for i in range(start, peers - 1, 2)]
        busy = {i for pair in pairs for i in pair}
        rounds.append(pairs + [(j, i) for i, j in pairs] + [(i, i) for i in range(peers) if i not in busy])
    return rounds


def exchange(first, last, axis):
    odd = lax.axis_index(axis) % 2 == 1
    near, far = pairings(lax.axis_size(axis))
    one = lax.ppermute(jnp.where(odd, first, last), axis, near)
    two = lax.ppermute(jnp.where(odd, last, first), axis, far)
    return one, two


def beside(one, two, axis):
    peers, index = lax.axis_size(axis), lax.axis_index(axis)
    odd = index % 2 == 1
    before = jnp.where(odd, one, two)
    after = jnp.where(odd, two, one)
    before = jnp.where(index == 0, jnp.zeros_like(before), before)
    after = jnp.where(index == peers - 1, jnp.zeros_like(after), after)
    return before, after


def by_origin(parts, axis, dim):
    peers, index = lax.axis_size(axis), lax.axis_index(axis)
    if peers == 2:
        return jnp.where(index == 0, jnp.concatenate(parts, dim), jnp.concatenate(parts[::-1], dim))
    stacked = jnp.stack(parts)
    order = (index - jnp.arange(peers)) % peers
    return jnp.concatenate([stacked[order[c]] for c in range(peers)], dim)


def swapped(piece, axis):
    peers, index = lax.axis_size(axis), lax.axis_index(axis)
    parts = [piece(index)]
    for s in range(1, peers):
        parts.append(lax.ppermute(piece((index + s) % peers), axis, [(i, (i + s) % peers) for i in range(peers)]))
    return parts


def to_columns(x, axis):
    own = x.shape[2] // lax.axis_size(axis)
    padded = jnp.pad(x, ((0, 0), (0, 0), (2, 2), (0, 0)))
    return by_origin(swapped(lambda i: lax.dynamic_slice_in_dim(padded, i * own, own + 4, 2), axis), axis, 3)


def stage_kernel(k1, k2, o1, o2, sems):
    copies = [pltpu.make_async_copy(k1, o1, sems.at[0]), pltpu.make_async_copy(k2, o2, sems.at[1])]
    for copy in copies:
        copy.start()
    for copy in copies:
        copy.wait()


def staged(k1, k2):
    return pl.pallas_call(
        stage_kernel,
        out_shape=[jax.ShapeDtypeStruct(k1.shape, k1.dtype), jax.ShapeDtypeStruct(k2.shape, k2.dtype)],
        in_specs=[ANY, ANY],
        out_specs=[VMEM, VMEM],
        scratch_shapes=[pltpu.SemaphoreType.DMA((2,))],
        cost_estimate=pl.CostEstimate(flops=0, bytes_accessed=2 * (k1.size + k2.size) * 2, transcendentals=0),
        compiler_params=pltpu.CompilerParams(vmem_limit_bytes=24 * 2**20),
        name="weights",
    )(k1, k2)


def spread(x, row, sides, info, x3, ef, e3, eb):
    H, Wp, C = x.shape
    own = Wp - 4
    for c in range(3):
        x3[row, :, :, c * C:(c + 1) * C] = x[:, 1 + c:1 + c + own, :]
    for s in range(sides):
        low, high = x[:, 0:3, :], x[:, Wp - 3:Wp, :]
        pick = jnp.where(info[4] == 0, high, low) if sides == 1 else (low, high)[s]
        pick = pick.astype(jnp.float32)
        for l in range(0, C, 128):
            for h in range(H):
                ef[s, l // 128, pl.ds(pl.multiple_of((row * H + h) * 8, 8), 3), :] = pick[h, :, l:l + 128]
            for c in range(3):
                e3[s, row, 0:H, c * C + l:c * C + l + 128] = ef[s, l // 128, pl.ds(row * H * 8 + c, H, stride=8), :]
        for b in range(3):
            eb[s, b, row] = e3[s, row, b:b + H, :].astype(jnp.bfloat16)


def hidden_rows(d, sides, info, global_row, x3, eb, k1, bias, store):
    H, own, C = x3.shape[1], x3.shape[2], x3.shape[3] // 3
    H1 = H - 2
    main = 2 * H1 * own
    acc = jnp.zeros((main + sides * 2 * H, C), jnp.float32)
    for a in range(3):
        for b in range(3):
            lhs = [x3[d + a:d + a + 2, b:b + H1].reshape(main, 3 * C)]
            lhs += [eb[s, b, d + a:d + a + 2].reshape(2 * H, 3 * C) for s in range(sides)]
            acc += jnp.dot(jnp.concatenate(lhs, 0), k1[a, b].reshape(3 * C, C), preferred_element_type=jnp.float32)
    acc = leaky(acc + bias)
    column = lax.broadcasted_iota(jnp.int32, (own, C), 0)
    none = jnp.zeros((1, C), jnp.float32)
    for q in range(2):
        rows = acc[q * H1 * own:(q + 1) * H1 * own].reshape(H1, own, C)
        ends = [acc[main + (s * 2 + q) * H:main + (s * 2 + q + 1) * H] for s in range(sides)]
        depth = global_row + q
        inside = jnp.logical_and(depth >= 0, depth < info[1])
        for h in range(H1):
            ok = inside
            if h == 0:
                ok = jnp.logical_and(ok, info[2] == 0)
            if h == H1 - 1:
                ok = jnp.logical_and(ok, info[3] == 0)
            row = jnp.where(ok, rows[h], 0.0)
            left, right = ends[0][h:h + 1], ends[sides - 1][h:h + 1]
            left = jnp.where(jnp.logical_and(ok, info[4] > 0), left, none)
            right = jnp.where(jnp.logical_and(ok, info[4] < info[5] - 1), right, none)
            store(q, h, 0, jnp.where(column == 0, left, pltpu.roll(row, 1, 0)).astype(jnp.bfloat16))
            store(q, h, 1, row.astype(jnp.bfloat16))
            store(q, h, 2, jnp.where(column == own - 1, right, pltpu.roll(row, own - 1, 0)).astype(jnp.bfloat16))


def feature_rows(d, h3, k2, bias, o_ref):
    H1, own, C = h3.shape[1], h3.shape[2], h3.shape[3] // 3
    H0 = H1 - 2
    acc = jnp.zeros((2 * H0 * own, C), jnp.float32)
    for a in range(3):
        for b in range(3):
            lhs = h3[d + a:d + a + 2, b:b + H0].reshape(2 * H0 * own, 3 * C)
            acc += jnp.dot(lhs, k2[a, b].reshape(3 * C, C), preferred_element_type=jnp.float32)
    o_ref[...] = leaky(acc + bias).astype(jnp.bfloat16).reshape(2, H0, own, C)


def near_kernel(sides, info, xc, xn, k1, b1, k2, b2, o_ref, keep, x3, ef, e3, eb, h3):
    D = xc.shape[0]
    C = xc.shape[3]
    odd = info[6]
    for d in range(D):
        spread(xc[d], 2 * odd + d, sides, info, x3, ef, e3, eb)
    for d in range(2):
        x = xn[d]
        x = jnp.where(info[7] == 0, x, jnp.zeros_like(x))
        spread(x, D * (1 - odd) + d, sides, info, x3, ef, e3, eb)
    first = info[0] - 1 + 2 * (1 - odd)

    for d in range(0, D, 2):
        def store(q, h, c, value, d=d):
            h3[d + q, h, :, c * C:(c + 1) * C] = value
        hidden_rows(d, sides, info, first + d, x3, eb, k1, b1[...], store)
    keep[...] = h3[pl.ds((D - 2) * odd, 2)]
    for d in range(0, D - 2, 2):
        feature_rows(d, h3, k2, b2[...], o_ref)


def far_kernel(sides, info, xc, xf, keep, k1, b1, k2, b2, o_ref, x3, ef, e3, eb, h3):
    D = xc.shape[0]
    C = xc.shape[3]
    odd = info[6]
    for d in range(2):
        spread(xc[(D - 2) * odd + d], 2 * (1 - odd) + d, sides, info, x3, ef, e3, eb)
    for d in range(2):
        x = xf[d]
        x = jnp.where(info[8] == 0, x, jnp.zeros_like(x))
        spread(x, 2 * odd + d, sides, info, x3, ef, e3, eb)
    first = info[0] - 1 + D * odd
    h3[pl.ds(2 * (1 - odd), 2)] = keep[...]

    def store(q, h, c, value):
        h3[2 * odd + q, h, :, c * C:(c + 1) * C] = value
    hidden_rows(0, sides, info, first, x3, eb, k1, b1[...], store)
    feature_rows(0, h3, k2, b2[...], o_ref)


def kernel_call(kernel, name, rows, sides, xc, keeps, operands):
    D, H, Wp, C = xc.shape
    own = Wp - 4
    out = [jax.ShapeDtypeStruct((2, H - 4, own, C), jnp.bfloat16)]
    if keeps:
        out.append(jax.ShapeDtypeStruct((2, H - 2, own, 3 * C), jnp.bfloat16))
    hid = (rows - 2) * (H - 2) * own
    return pl.pallas_call(
        functools.partial(kernel, sides),
        out_shape=out,
        in_specs=[SMEM] + [VMEM] * (len(operands) - 1),
        out_specs=[VMEM] * len(out),
        scratch_shapes=[
            pltpu.VMEM((rows, H, own, 3 * C), jnp.bfloat16),
            pltpu.VMEM((sides, C // 128, rows * H * 8, 128), jnp.float32),
            pltpu.VMEM((sides, rows, 2 * H, 3 * C), jnp.float32),
            pltpu.VMEM((sides, 3, rows, H, 3 * C), jnp.bfloat16),
            pltpu.VMEM((4, H - 2, own, 3 * C), jnp.bfloat16),
        ],
        compiler_params=pltpu.CompilerParams(vmem_limit_bytes=24 * 2**20),
        cost_estimate=pl.CostEstimate(flops=2 * 27 * C * C * (hid + 2 * (H - 4) * own), bytes_accessed=2**20, transcendentals=0),
        name=name,
    )(*operands)


def body(volume, kernel_one, bias_one, kernel_two, bias_two):
    k1, k2 = staged(kernel_one, kernel_two)
    b1, b2 = bias_one.reshape(1, -1), bias_two.reshape(1, -1)
    d, h, f = (lax.axis_index(a) for a in ("depth", "height", "filt"))
    nd, nh, nf = (lax.axis_size(a) for a in ("depth", "height", "filt"))
    rows = volume.shape[0]
    odd = d % 2
    info = jnp.stack([
        d * rows, jnp.int32(nd * rows), (h == 0).astype(jnp.int32), (h == nh - 1).astype(jnp.int32), f, jnp.int32(nf), odd,
        jnp.logical_and(odd == 0, d == nd - 1).astype(jnp.int32),
        jnp.where(odd == 1, d == nd - 1, d == 0).astype(jnp.int32),
    ])
    sides = 1 if nf == 2 else 2

    whole = to_columns(volume, "filt")
    before, after = beside(*exchange(whole[:, :2], whole[:, -2:], "height"), "height")
    tall = jnp.concatenate([before, whole, after], 1)
    near, far = exchange(tall[:2], tall[-2:], "depth")
    out_near, keep = kernel_call(near_kernel, "near", rows + 2, sides, tall, True, (info, tall, near, k1, b1, k2, b2))
    shard = volume.shape[3]
    near_parts = swapped(lambda i: lax.dynamic_slice_in_dim(out_near, i * shard, shard, 3), "filt")
    out_far, = kernel_call(far_kernel, "far", 4, sides, tall, False, (info, tall, far, keep, k1, b1, k2, b2))
    far_parts = swapped(lambda i: lax.dynamic_slice_in_dim(out_far, i * shard, shard, 3), "filt")
    out_near, out_far = by_origin(near_parts, "filt", 2), by_origin(far_parts, "filt", 2)
    return jnp.where(odd == 1, jnp.concatenate([out_near, out_far], 0), jnp.concatenate([out_far, out_near], 0))


def solution(mesh):
    in_specs = (P("depth", "height", None, "filt"), P(), P(), P(), P())
    out_specs = P("depth", "height", None, "filt")
    return jax.shard_map(body, mesh=mesh, in_specs=in_specs, out_specs=out_specs, check_vma=False)
```

```python
import functools

import jax
import jax.numpy as jnp
from jax import lax
from jax.experimental import pallas as pl
from jax.experimental.pallas import tpu as pltpu
from jax.sharding import PartitionSpec as P

VMEM = pl.BlockSpec(memory_space=pltpu.VMEM)
SMEM = pl.BlockSpec(memory_space=pltpu.SMEM)
HBM = pl.BlockSpec(memory_space=pltpu.HBM)


def leaky(value):
    return jnp.where(value > 0, value, 0.3 * value)


def pairings(peers):
    rounds = []
    for start in (0, 1):
        pairs = [(i, i + 1) for i in range(start, peers - 1, 2)]
        busy = {i for pair in pairs for i in pair}
        rounds.append(pairs + [(j, i) for i, j in pairs] + [(i, i) for i in range(peers) if i not in busy])
    return rounds


def exchange(first, last, axis):
    odd = lax.axis_index(axis) % 2 == 1
    near, far = pairings(lax.axis_size(axis))
    one = lax.ppermute(jnp.where(odd, first, last), axis, near)
    two = lax.ppermute(jnp.where(odd, last, first), axis, far)
    return one, two


def beside(one, two, axis):
    peers, index = lax.axis_size(axis), lax.axis_index(axis)
    odd = index % 2 == 1
    before = jnp.where(odd, one, two)
    after = jnp.where(odd, two, one)
    before = jnp.where(index == 0, jnp.zeros_like(before), before)
    after = jnp.where(index == peers - 1, jnp.zeros_like(after), after)
    return before, after


def by_origin(parts, axis, dim):
    peers, index = lax.axis_size(axis), lax.axis_index(axis)
    if peers == 2:
        return jnp.where(index == 0, jnp.concatenate(parts, dim), jnp.concatenate(parts[::-1], dim))
    stacked = jnp.stack(parts)
    order = (index - jnp.arange(peers)) % peers
    return jnp.concatenate([stacked[order[c]] for c in range(peers)], dim)


def swapped(piece, axis):
    peers, index = lax.axis_size(axis), lax.axis_index(axis)
    parts = [piece(index)]
    for s in range(1, peers):
        parts.append(lax.ppermute(piece((index + s) % peers), axis, [(i, (i + s) % peers) for i in range(peers)]))
    return parts


def in_order(parts, axis):
    return by_origin(parts, axis, 3)


def gathered(x, columns, rows):
    nc, nr = lax.axis_size(columns), lax.axis_size(rows)
    c, r = lax.axis_index(columns), lax.axis_index(rows)
    own = x.shape[2] // nc
    odd = r % 2 == 1
    padded = jnp.pad(x, ((0, 0), (0, 0), (2, 2), (0, 0)))
    windows = [lax.dynamic_slice_in_dim(padded, (c + s) % nc * own, own + 4, 2) for s in range(nc)]
    windows = lax.optimization_barrier(windows)
    parts, ones, twos = [windows[0]], [], []
    near, far = pairings(nr)
    for s in range(1, nc):
        parts.append(lax.ppermute(windows[s], columns, [(i, (i + s) % nc) for i in range(nc)]))
    for s in range(nc):
        first, last = windows[s][:, :2], windows[s][:, -2:]
        for to, edge, pairs in ((ones, jnp.where(odd, first, last), near), (twos, jnp.where(odd, last, first), far)):
            moves = [(i * nc + k, j * nc + (k + s) % nc) for i, j in pairs for k in range(nc)]
            to.append(lax.ppermute(edge, (rows, columns), moves))
    one, two = in_order(ones, columns), in_order(twos, columns)
    before, after = beside(one, two, rows)
    return jnp.concatenate([before, in_order(parts, columns), after], 1)


def spread(source, rows, at, sides, info, x3, ef, e3, eb):
    H, Wp, C = source.shape[1:]
    own = Wp - 4

    def step(d, carry):
        x, row = source[d], at + d
        for c in range(3):
            x3[row, :, :, c * C:(c + 1) * C] = x[:, 1 + c:1 + c + own, :]
        for s in range(sides):
            low, high = x[:, 0:3, :], x[:, Wp - 3:Wp, :]
            pick = jnp.where(info[4] == 0, high, low) if sides == 1 else (low, high)[s]
            pick = pick.astype(jnp.float32)
            for l in range(0, C, 128):
                for h in range(H):
                    ef[s, l // 128, pl.ds(h * 8, 3), :] = pick[h, :, l:l + 128]
                for c in range(3):
                    e3[s, 0:H, c * C + l:c * C + l + 128] = ef[s, l // 128, pl.ds(c, H, stride=8), :]
            for b in range(3):
                eb[s, b, row] = e3[s, b:b + H, :].astype(jnp.bfloat16)
        return carry

    lax.fori_loop(0, rows, step, 0)


def clear(rows, at, x3, eb):
    for d in range(rows):
        x3[at + d] = jnp.zeros(x3.shape[1:], x3.dtype)
        for s in range(eb.shape[0]):
            for b in range(3):
                eb[s, b, at + d] = jnp.zeros(eb.shape[3:], eb.dtype)


def hidden_sums(d, sides, x3, eb, k1, bias, raw, ready):
    H, own, C = x3.shape[1], x3.shape[2], x3.shape[3] // 3
    H1 = H - 2
    main = 2 * H1 * own
    acc = jnp.zeros((main + sides * 2 * H, C), jnp.float32)
    for a in range(3):
        ready(a)
        for b in range(3):
            lhs = [x3[pl.ds(d + a, 2), b:b + H1].reshape(main, 3 * C)]
            lhs += [eb[s, b, pl.ds(d + a, 2)].reshape(2 * H, 3 * C) for s in range(sides)]
            acc += jnp.dot(jnp.concatenate(lhs, 0), k1[a, b].reshape(3 * C, C), preferred_element_type=jnp.float32)
    raw[...] = leaky(acc + bias)


def hidden_rows(at, depth, sides, info, own, H, raw, h3):
    C = raw.shape[1]
    H1 = H - 2
    main = 2 * H1 * own
    column = lax.broadcasted_iota(jnp.int32, (own, C), 0)
    none = jnp.zeros((1, C), jnp.float32)

    def step(i, carry):
        q, h = i // H1, i % H1
        ok = jnp.logical_and(depth + q >= 0, depth + q < info[1])
        ok = jnp.logical_and(ok, jnp.logical_or(h > 0, info[2] == 0))
        ok = jnp.logical_and(ok, jnp.logical_or(h < H1 - 1, info[3] == 0))
        row = jnp.where(ok, raw[pl.ds(pl.multiple_of(i * own, 8), own), :], 0.0)
        ends = [raw[pl.ds(main + (s * 2 + q) * H + h, 1), :] for s in range(sides)]
        left = jnp.where(jnp.logical_and(ok, info[4] > 0), ends[0], none)
        right = jnp.where(jnp.logical_and(ok, info[4] < info[5] - 1), ends[sides - 1], none)
        h3[at + q, h, :, 0:C] = jnp.where(column == 0, left, pltpu.roll(row, 1, 0)).astype(jnp.bfloat16)
        h3[at + q, h, :, C:2 * C] = row.astype(jnp.bfloat16)
        h3[at + q, h, :, 2 * C:] = jnp.where(column == own - 1, right, pltpu.roll(row, own - 1, 0)).astype(jnp.bfloat16)
        return carry

    lax.fori_loop(0, 2 * H1, step, 0)


def feature_rows(h3, k2, bias, o_ref, ready):
    H1, own, C = h3.shape[1], h3.shape[2], h3.shape[3] // 3
    H0 = H1 - 2
    acc = jnp.zeros((2 * H0 * own, C), jnp.float32)
    for a in range(3):
        ready(a)
        for b in range(3):
            lhs = h3[a:a + 2, b:b + H0].reshape(2 * H0 * own, 3 * C)
            acc += jnp.dot(lhs, k2[a, b].reshape(3 * C, C), preferred_element_type=jnp.float32)
    o_ref[...] = leaky(acc + bias).astype(jnp.bfloat16).reshape(2, H0, own, C)


def fetched(k1h, k2h, k1, k2, sems):
    copies = [pltpu.make_async_copy(k1h.at[a], k1.at[a], sems.at[a]) for a in range(3)]
    copies += [pltpu.make_async_copy(k2h.at[a], k2.at[a], sems.at[3 + a]) for a in range(3)]
    for copy in copies:
        copy.start()
    return copies


def near_kernel(sides, info, xc, xn, k1h, b1, k2h, b2, o_ref, keep, x3, ef, e3, eb, h3, raw, k1, k2, sems):
    copies = fetched(k1h, k2h, k1, k2, sems)
    D, H, own = xc.shape[0], xc.shape[1], xc.shape[2] - 4
    odd = info[6]
    scratch = (x3, ef, e3, eb)
    spread(xc, D, 2 * odd, sides, info, *scratch)
    spread(xn, 2, D * (1 - odd), sides, info, *scratch)

    @pl.when(info[7] > 0)
    def _():
        clear(2, D * (1 - odd), x3, eb)

    def step(t, carry):
        def ready(a):
            @pl.when(t == 0)
            def _():
                copies[a].wait()
        hidden_sums(2 * t, sides, x3, eb, k1, b1[...], raw, ready)
        hidden_rows(2 * t, info[0] - 1 + 2 * (1 - odd) + 2 * t, sides, info, own, H, raw, h3)
        return carry

    lax.fori_loop(0, D // 2, step, 0)
    keep[...] = h3[pl.ds((D - 2) * odd, 2)]
    for a in range(3):
        copies[3 + a].wait()

    @pl.when(info[5] > 0)
    def _():
        feature_rows(h3, k2, b2[...], o_ref, lambda a: None)


def far_kernel(sides, info, xc, xf, keep, k1h, b1, k2h, b2, o_ref, x3, ef, e3, eb, h3, raw, k1, k2, sems):
    copies = fetched(k1h, k2h, k1, k2, sems)
    D, H, own = xc.shape[0], xc.shape[1], xc.shape[2] - 4
    odd = info[6]
    scratch = (x3, ef, e3, eb)
    spread(xc.at[pl.ds((D - 2) * odd, 2)], 2, 2 * (1 - odd), sides, info, *scratch)
    spread(xf, 2, 2 * odd, sides, info, *scratch)

    @pl.when(info[8] > 0)
    def _():
        clear(2, 2 * odd, x3, eb)

    h3[pl.ds(2 * (1 - odd), 2)] = keep[...]

    hidden_sums(0, sides, x3, eb, k1, b1[...], raw, lambda a: copies[a].wait())
    hidden_rows(2 * odd, info[0] - 1 + D * odd, sides, info, own, H, raw, h3)

    feature_rows(h3, k2, b2[...], o_ref, lambda a: copies[3 + a].wait())


def kernel_call(kernel, name, rows, sides, xc, near, operands):
    D, H, Wp, C = xc.shape
    own = Wp - 4
    out = [jax.ShapeDtypeStruct((2, H - 4, own, C), jnp.bfloat16)]
    scratch = [
        pltpu.VMEM((rows, H, own, 3 * C), jnp.bfloat16),
        pltpu.VMEM((sides, C // 128, H * 8, 128), jnp.float32),
        pltpu.VMEM((sides, 2 * H, 3 * C), jnp.float32),
        pltpu.VMEM((sides, 3, rows, H, 3 * C), jnp.bfloat16),
        pltpu.VMEM((4, H - 2, own, 3 * C), jnp.bfloat16),
        pltpu.VMEM((2 * (H - 2) * own + sides * 2 * H, C), jnp.float32),
        pltpu.VMEM((3, 3, 3, C, C), jnp.bfloat16),
        pltpu.VMEM((3, 3, 3, C, C), jnp.bfloat16),
        pltpu.SemaphoreType.DMA((6,)),
    ]
    specs = [SMEM] + [VMEM] * (len(operands) - 1)
    specs[-4] = specs[-2] = HBM
    if near:
        out += [jax.ShapeDtypeStruct((2, H - 2, own, 3 * C), jnp.bfloat16)]
    hid = (rows - 2) * (H - 2) * own
    return pl.pallas_call(
        functools.partial(kernel, sides),
        out_shape=out,
        in_specs=specs,
        out_specs=[VMEM] * len(out),
        scratch_shapes=scratch,
        compiler_params=pltpu.CompilerParams(vmem_limit_bytes=56 * 2**20),
        cost_estimate=pl.CostEstimate(flops=2 * 27 * C * C * (hid + 2 * (H - 4) * own), bytes_accessed=2**20, transcendentals=0),
        name=name,
    )(*operands)


def body(volume, kernel_one, bias_one, kernel_two, bias_two):
    b1, b2 = bias_one.reshape(1, -1), bias_two.reshape(1, -1)
    d, h, f = (lax.axis_index(a) for a in ("depth", "height", "filt"))
    nd, nh, nf = (lax.axis_size(a) for a in ("depth", "height", "filt"))
    rows = volume.shape[0]
    odd = d % 2
    info = jnp.stack([
        d * rows, jnp.int32(nd * rows), (h == 0).astype(jnp.int32), (h == nh - 1).astype(jnp.int32), f, jnp.int32(nf), odd,
        jnp.logical_and(odd == 0, d == nd - 1).astype(jnp.int32),
        jnp.where(odd == 1, d == nd - 1, d == 0).astype(jnp.int32),
    ])
    sides = 1 if nf == 2 else 2

    tall = gathered(volume, "filt", "height")
    near, far = exchange(tall[:2], tall[-2:], "depth")
    out_near, keep = kernel_call(near_kernel, "near", rows + 2, sides, tall, True, (info, tall, near, kernel_one, b1, kernel_two, b2))
    shard = volume.shape[3]
    near_parts = swapped(lambda i: lax.dynamic_slice_in_dim(out_near, i * shard, shard, 3), "filt")
    out_far, = kernel_call(far_kernel, "far", 4, sides, tall, False, (info, tall, far, keep, kernel_one, b1, kernel_two, b2))
    far_parts = swapped(lambda i: lax.dynamic_slice_in_dim(out_far, i * shard, shard, 3), "filt")
    out_near, out_far = by_origin(near_parts, "filt", 2), by_origin(far_parts, "filt", 2)
    return jnp.where(odd == 1, jnp.concatenate([out_near, out_far], 0), jnp.concatenate([out_far, out_near], 0))


def solution(mesh):
    in_specs = (P("depth", "height", None, "filt"), P(), P(), P(), P())
    out_specs = P("depth", "height", None, "filt")
    return jax.shard_map(body, mesh=mesh, in_specs=in_specs, out_specs=out_specs, check_vma=False)
```

```python
import functools

import jax
import jax.numpy as jnp
from jax import lax
from jax.experimental import pallas as pl
from jax.experimental.pallas import tpu as pltpu
from jax.sharding import PartitionSpec as P

VMEM = pl.BlockSpec(memory_space=pltpu.VMEM)
HBM = pl.BlockSpec(memory_space=pltpu.HBM)


def leaky(value):
    return jnp.where(value > 0, value, 0.3 * value)


def pairings(peers):
    rounds = []
    for start in (0, 1):
        pairs = [(i, i + 1) for i in range(start, peers - 1, 2)]
        busy = {i for pair in pairs for i in pair}
        rounds.append(pairs + [(j, i) for i, j in pairs] + [(i, i) for i in range(peers) if i not in busy])
    return rounds


def exchange(first, last, axis):
    odd = lax.axis_index(axis) % 2 == 1
    near, far = pairings(lax.axis_size(axis))
    one = lax.ppermute(jnp.where(odd, first, last), axis, near)
    two = lax.ppermute(jnp.where(odd, last, first), axis, far)
    return one, two


def beside(one, two, axis):
    peers, index = lax.axis_size(axis), lax.axis_index(axis)
    odd = index % 2 == 1
    before = jnp.where(odd, one, two)
    after = jnp.where(odd, two, one)
    before = jnp.where(index == 0, jnp.zeros_like(before), before)
    after = jnp.where(index == peers - 1, jnp.zeros_like(after), after)
    return before, after


def by_origin(parts, axis, dim):
    peers, index = lax.axis_size(axis), lax.axis_index(axis)
    if peers == 2:
        return jnp.where(index == 0, jnp.concatenate(parts, dim), jnp.concatenate(parts[::-1], dim))
    stacked = jnp.stack(parts)
    order = (index - jnp.arange(peers)) % peers
    return jnp.concatenate([stacked[order[c]] for c in range(peers)], dim)


def swapped(piece, axis):
    peers, index = lax.axis_size(axis), lax.axis_index(axis)
    parts = [piece(index)]
    for s in range(1, peers):
        parts.append(lax.ppermute(piece((index + s) % peers), axis, [(i, (i + s) % peers) for i in range(peers)]))
    return parts


def in_order(parts, axis):
    return by_origin(parts, axis, 3)


def gathered(x, columns, rows):
    nc, nr = lax.axis_size(columns), lax.axis_size(rows)
    c, r = lax.axis_index(columns), lax.axis_index(rows)
    own = x.shape[2] // nc
    odd = r % 2 == 1
    padded = jnp.pad(x, ((0, 0), (0, 0), (2, 2), (0, 0)))
    windows = [lax.dynamic_slice_in_dim(padded, (c + s) % nc * own, own + 4, 2) for s in range(nc)]
    windows = lax.optimization_barrier(windows)
    parts, ones, twos = [windows[0]], [], []
    near, far = pairings(nr)
    for s in range(1, nc):
        parts.append(lax.ppermute(windows[s], columns, [(i, (i + s) % nc) for i in range(nc)]))
    for s in range(nc):
        first, last = windows[s][:, :2], windows[s][:, -2:]
        for to, edge, pairs in ((ones, jnp.where(odd, first, last), near), (twos, jnp.where(odd, last, first), far)):
            moves = [(i * nc + k, j * nc + (k + s) % nc) for i, j in pairs for k in range(nc)]
            to.append(lax.ppermute(edge, (rows, columns), moves))
    one, two = in_order(ones, columns), in_order(twos, columns)
    before, after = beside(one, two, rows)
    return jnp.concatenate([before, in_order(parts, columns), after], 1)


def spread(source, rows, at, sides, info, x3, ef, e3, eb):
    H, Wp, C = source.shape[1:]
    own = Wp - 4

    def step(d):
        x, row = source[d], at + d
        for c in range(3):
            x3[row, :, :, c * C:(c + 1) * C] = x[:, 1 + c:1 + c + own, :]
        for s in range(sides):
            low, high = x[:, 0:3, :], x[:, Wp - 3:Wp, :]
            pick = jnp.where(info[4] == 0, high, low) if sides == 1 else (low, high)[s]
            pick = pick.astype(jnp.float32)
            for l in range(0, C, 128):
                for h in range(H):
                    ef[s, l // 128, pl.ds(h * 8, 3), :] = pick[h, :, l:l + 128]
                for c in range(3):
                    e3[s, 0:H, c * C + l:c * C + l + 128] = ef[s, l // 128, pl.ds(c, H, stride=8), :]
            for b in range(3):
                eb[s, b, row] = e3[s, b:b + H, :].astype(jnp.bfloat16)

    for d in range(rows):
        step(d)


def clear(rows, at, x3, eb):
    for d in range(rows):
        x3[at + d] = jnp.zeros(x3.shape[1:], x3.dtype)
        for s in range(eb.shape[0]):
            for b in range(3):
                eb[s, b, at + d] = jnp.zeros(eb.shape[3:], eb.dtype)


def hidden_sums(d, sides, x3, eb, k1, bias, raw, ready):
    H, own, C = x3.shape[1], x3.shape[2], x3.shape[3] // 3
    H1 = H - 2
    main = 2 * H1 * own
    acc = jnp.zeros((main + sides * 2 * H, C), jnp.float32)
    for a in range(3):
        ready(a)
        for b in range(3):
            lhs = [x3[pl.ds(d + a, 2), b:b + H1].reshape(main, 3 * C)]
            lhs += [eb[s, b, pl.ds(d + a, 2)].reshape(2 * H, 3 * C) for s in range(sides)]
            acc += jnp.dot(jnp.concatenate(lhs, 0), k1[a, b].reshape(3 * C, C), preferred_element_type=jnp.float32)
    raw[...] = leaky(acc + bias)


def hidden_rows(at, depth, sides, info, own, H, raw, h3):
    C = raw.shape[1]
    H1 = H - 2
    main = 2 * H1 * own
    column = lax.broadcasted_iota(jnp.int32, (own, C), 0)
    none = jnp.zeros((1, C), jnp.float32)

    def step(i):
        q, h = i // H1, i % H1
        ok = jnp.logical_and(depth + q >= 0, depth + q < info[1])
        ok = jnp.logical_and(ok, jnp.logical_or(h > 0, info[2] == 0))
        ok = jnp.logical_and(ok, jnp.logical_or(h < H1 - 1, info[3] == 0))
        row = jnp.where(ok, raw[pl.ds(pl.multiple_of(i * own, 8), own), :], 0.0)
        ends = [raw[pl.ds(main + (s * 2 + q) * H + h, 1), :] for s in range(sides)]
        left = jnp.where(jnp.logical_and(ok, info[4] > 0), ends[0], none)
        right = jnp.where(jnp.logical_and(ok, info[4] < info[5] - 1), ends[sides - 1], none)
        h3[at + q, h, :, 0:C] = jnp.where(column == 0, left, pltpu.roll(row, 1, 0)).astype(jnp.bfloat16)
        h3[at + q, h, :, C:2 * C] = row.astype(jnp.bfloat16)
        h3[at + q, h, :, 2 * C:] = jnp.where(column == own - 1, right, pltpu.roll(row, own - 1, 0)).astype(jnp.bfloat16)

    for i in range(2 * H1):
        step(i)


def feature_rows(h3, k2, bias, o_ref, ready):
    H1, own, C = h3.shape[1], h3.shape[2], h3.shape[3] // 3
    H0 = H1 - 2
    acc = jnp.zeros((2 * H0 * own, C), jnp.float32)
    for a in range(3):
        ready(a)
        for b in range(3):
            lhs = h3[a:a + 2, b:b + H0].reshape(2 * H0 * own, 3 * C)
            acc += jnp.dot(lhs, k2[a, b].reshape(3 * C, C), preferred_element_type=jnp.float32)
    o_ref[...] = leaky(acc + bias).astype(jnp.bfloat16).reshape(2, H0, own, C)


def spread(source, rows, at, sides, info, x3, ef, e3, eb):
    H, Wp, C = source.shape[1:]
    own = Wp - 4

    def step(d):
        x, row = source[d], at + d
        for c in range(3):
            x3[row, :, :, c * C:(c + 1) * C] = x[:, 1 + c:1 + c + own, :]
        for s in range(sides):
            low, high = x[:, 0:3, :], x[:, Wp - 3:Wp, :]
            pick = jnp.where(info[4] == 0, high, low) if sides == 1 else (low, high)[s]
            pick = pick.astype(jnp.float32)
            for l in range(0, C, 128):
                for h in range(H):
                    ef[s, l // 128, pl.ds(h * 8, 3), :] = pick[h, :, l:l + 128]
                for c in range(3):
                    e3[s, 0:H, c * C + l:c * C + l + 128] = ef[s, l // 128, pl.ds(c, H, stride=8), :]
            for b in range(3):
                eb[s, b, row] = e3[s, b:b + H, :].astype(jnp.bfloat16)

    for d in range(rows):
        step(d)


def clear(rows, at, x3, eb):
    for d in range(rows):
        x3[at + d] = jnp.zeros(x3.shape[1:], x3.dtype)
        for s in range(eb.shape[0]):
            for b in range(3):
                eb[s, b, at + d] = jnp.zeros(eb.shape[3:], eb.dtype)


def hidden_sums(d, sides, x3, eb, k1, bias, raw, ready):
    H, own, C = x3.shape[1], x3.shape[2], x3.shape[3] // 3
    H1 = H - 2
    main = 2 * H1 * own
    acc = jnp.zeros((main + sides * 2 * H, C), jnp.float32)
    for a in range(3):
        ready(a)
        for b in range(3):
            lhs = [x3[pl.ds(d + a, 2), b:b + H1].reshape(main, 3 * C)]
            lhs += [eb[s, b, pl.ds(d + a, 2)].reshape(2 * H, 3 * C) for s in range(sides)]
            acc += jnp.dot(jnp.concatenate(lhs, 0), k1[a, b].reshape(3 * C, C), preferred_element_type=jnp.float32)
    raw[...] = leaky(acc + bias)


def hidden_rows(at, depth, sides, info, own, H, raw, h3):
    C = raw.shape[1]
    H1 = H - 2
    main = 2 * H1 * own
    column = lax.broadcasted_iota(jnp.int32, (own, C), 0)
    none = jnp.zeros((1, C), jnp.float32)

    def step(i):
        q, h = i // H1, i % H1
        ok = jnp.logical_and(depth + q >= 0, depth + q < info[1])
        ok = jnp.logical_and(ok, jnp.logical_or(h > 0, info[2] == 0))
        ok = jnp.logical_and(ok, jnp.logical_or(h < H1 - 1, info[3] == 0))
        row = jnp.where(ok, raw[pl.ds(pl.multiple_of(i * own, 8), own), :], 0.0)
        ends = [raw[pl.ds(main + (s * 2 + q) * H + h, 1), :] for s in range(sides)]
        left = jnp.where(jnp.logical_and(ok, info[4] > 0), ends[0], none)
        right = jnp.where(jnp.logical_and(ok, info[4] < info[5] - 1), ends[sides - 1], none)
        h3[at + q, h, :, 0:C] = jnp.where(column == 0, left, pltpu.roll(row, 1, 0)).astype(jnp.bfloat16)
        h3[at + q, h, :, C:2 * C] = row.astype(jnp.bfloat16)
        h3[at + q, h, :, 2 * C:] = jnp.where(column == own - 1, right, pltpu.roll(row, own - 1, 0)).astype(jnp.bfloat16)

    for i in range(2 * H1):
        step(i)


def feature_rows(h3, k2, bias, o_ref, ready):
    H1, own, C = h3.shape[1], h3.shape[2], h3.shape[3] // 3
    H0 = H1 - 2
    acc = jnp.zeros((2 * H0 * own, C), jnp.float32)
    for a in range(3):
        ready(a)
        for b in range(3):
            lhs = h3[a:a + 2, b:b + H0].reshape(2 * H0 * own, 3 * C)
            acc += jnp.dot(lhs, k2[a, b].reshape(3 * C, C), preferred_element_type=jnp.float32)
    o_ref[...] = leaky(acc + bias).astype(jnp.bfloat16).reshape(2, H0, own, C)


def places(rows):
    d, h, f = (lax.axis_index(a) for a in ("depth", "height", "filt"))
    nd, nh, nf = (lax.axis_size(a) for a in ("depth", "height", "filt"))
    odd = lax.rem(d, 2)
    end = (d == nd - 1).astype(jnp.int32)
    start = (d == 0).astype(jnp.int32)
    return (d * rows, nd * rows, (h == 0).astype(jnp.int32), (h == nh - 1).astype(jnp.int32), f, nf, odd,
            end * (1 - odd), jnp.where(odd == 1, end, start))


def near_kernel(sides, xc, xn, k1h, b1, k2h, b2, o_ref, keep, k1, k2, x3, ef, e3, eb, h3, raw, sems):
    copies = [pltpu.make_async_copy(k1h.at[a], k1.at[a], sems.at[a]) for a in range(3)]
    copies += [pltpu.make_async_copy(k2h.at[a], k2.at[a], sems.at[3 + a]) for a in range(3)]
    for copy in copies[:2]:
        copy.start()

    def take(i):
        copies[i].wait()
        if i + 2 < len(copies):
            copies[i + 2].start()

    D, H, own = xc.shape[0], xc.shape[1], xc.shape[2] - 4
    info = places(D)
    odd = info[6]
    scratch = (x3, ef, e3, eb)
    spread(xc, D, 2 * odd, sides, info, *scratch)
    spread(xn, 2, D * (1 - odd), sides, info, *scratch)

    @pl.when(info[7] > 0)
    def _():
        clear(2, D * (1 - odd), x3, eb)

    for t in range(0, D, 2):
        hidden_sums(t, sides, x3, eb, k1, b1[...], raw, (lambda a: take(a)) if t == 0 else (lambda a: None))
        hidden_rows(t, info[0] - 1 + 2 * (1 - odd) + t, sides, info, own, H, raw, h3)
    keep[...] = h3[pl.ds((D - 2) * odd, 2)]
    for a in range(3):
        take(3 + a)

    @pl.when(odd >= 0)
    def _():
        feature_rows(h3, k2, b2[...], o_ref, lambda a: None)


def far_kernel(sides, xc, xf, keep, k1, b1, k2, b2, o_ref, x3, ef, e3, eb, h3, raw):
    D, H, own = xc.shape[0], xc.shape[1], xc.shape[2] - 4
    info = places(D)
    odd = info[6]
    scratch = (x3, ef, e3, eb)
    spread(xc.at[pl.ds((D - 2) * odd, 2)], 2, 2 * (1 - odd), sides, info, *scratch)
    spread(xf, 2, 2 * odd, sides, info, *scratch)

    @pl.when(info[8] > 0)
    def _():
        clear(2, 2 * odd, x3, eb)

    h3[pl.ds(2 * (1 - odd), 2)] = keep[...]

    @pl.when(odd >= 0)
    def _():
        hidden_sums(0, sides, x3, eb, k1, b1[...], raw, lambda a: None)
    hidden_rows(2 * odd, info[0] - 1 + D * odd, sides, info, own, H, raw, h3)

    @pl.when(odd >= 0)
    def _():
        feature_rows(h3, k2, b2[...], o_ref, lambda a: None)


def kernel_call(kernel, name, rows, sides, xc, near, operands):
    D, H, Wp, C = xc.shape
    own = Wp - 4
    weights = jax.ShapeDtypeStruct((3, 3, 3, C, C), jnp.bfloat16)
    out = [jax.ShapeDtypeStruct((2, H - 4, own, C), jnp.bfloat16)]
    scratch = [
        pltpu.VMEM((rows, H, own, 3 * C), jnp.bfloat16),
        pltpu.VMEM((sides, C // 128, H * 8, 128), jnp.float32),
        pltpu.VMEM((sides, 2 * H, 3 * C), jnp.float32),
        pltpu.VMEM((sides, 3, rows, H, 3 * C), jnp.bfloat16),
        pltpu.VMEM((4, H - 2, own, 3 * C), jnp.bfloat16),
        pltpu.VMEM((2 * (H - 2) * own + sides * 2 * H, C), jnp.float32),
    ]
    specs = [VMEM] * len(operands)
    if near:
        out += [jax.ShapeDtypeStruct((2, H - 2, own, 3 * C), jnp.bfloat16), weights, weights]
        scratch.append(pltpu.SemaphoreType.DMA((6,)))
        specs[2] = specs[4] = HBM
    hid = (rows - 2) * (H - 2) * own
    return pl.pallas_call(
        functools.partial(kernel, sides),
        out_shape=out,
        in_specs=specs,
        out_specs=[VMEM] * len(out),
        scratch_shapes=scratch,
        compiler_params=pltpu.CompilerParams(vmem_limit_bytes=(43 if near else 24) * 2**20),
        cost_estimate=pl.CostEstimate(flops=2 * 27 * C * C * (hid + 2 * (H - 4) * own), bytes_accessed=2**20, transcendentals=0),
        name=name,
    )(*operands)


def body(volume, kernel_one, bias_one, kernel_two, bias_two):
    b1, b2 = bias_one.reshape(1, -1), bias_two.reshape(1, -1)
    rows, odd = volume.shape[0], lax.axis_index("depth") % 2
    sides = 1 if lax.axis_size("filt") == 2 else 2

    tall = gathered(volume, "filt", "height")
    near, far = exchange(tall[:2], tall[-2:], "depth")
    out_near, keep, k1, k2 = kernel_call(near_kernel, "near", rows + 2, sides, tall, True, (tall, near, kernel_one, b1, kernel_two, b2))
    shard = volume.shape[3]
    near_parts = swapped(lambda i: lax.dynamic_slice_in_dim(out_near, i * shard, shard, 3), "filt")
    out_far, = kernel_call(far_kernel, "far", 4, sides, tall, False, (tall, far, keep, k1, b1, k2, b2))
    far_parts = swapped(lambda i: lax.dynamic_slice_in_dim(out_far, i * shard, shard, 3), "filt")
    out_near, out_far = by_origin(near_parts, "filt", 2), by_origin(far_parts, "filt", 2)
    return jnp.where(odd == 1, jnp.concatenate([out_near, out_far], 0), jnp.concatenate([out_far, out_near], 0))


def solution(mesh):
    in_specs = (P("depth", "height", None, "filt"), P(), P(), P(), P())
    out_specs = P("depth", "height", None, "filt")
    return jax.shard_map(body, mesh=mesh, in_specs=in_specs, out_specs=out_specs, check_vma=False)
```

```python
import functools

import jax
import jax.numpy as jnp
from jax import lax
from jax.experimental import pallas as pl
from jax.experimental.pallas import tpu as pltpu
from jax.sharding import PartitionSpec as P

VMEM = pl.BlockSpec(memory_space=pltpu.VMEM)
HBM = pl.BlockSpec(memory_space=pltpu.HBM)


def leaky(value):
    return jnp.where(value > 0, value, 0.3 * value)


def pairings(peers):
    rounds = []
    for start in (0, 1):
        pairs = [(i, i + 1) for i in range(start, peers - 1, 2)]
        busy = {i for pair in pairs for i in pair}
        rounds.append(pairs + [(j, i) for i, j in pairs] + [(i, i) for i in range(peers) if i not in busy])
    return rounds


def exchange(first, last, axis):
    odd = lax.axis_index(axis) % 2 == 1
    near, far = pairings(lax.axis_size(axis))
    one = lax.ppermute(jnp.where(odd, first, last), axis, near)
    two = lax.ppermute(jnp.where(odd, last, first), axis, far)
    return one, two


def beside(one, two, axis):
    peers, index = lax.axis_size(axis), lax.axis_index(axis)
    odd = index % 2 == 1
    before = jnp.where(odd, one, two)
    after = jnp.where(odd, two, one)
    before = jnp.where(index == 0, jnp.zeros_like(before), before)
    after = jnp.where(index == peers - 1, jnp.zeros_like(after), after)
    return before, after


def by_origin(parts, axis, dim):
    peers, index = lax.axis_size(axis), lax.axis_index(axis)
    if peers == 2:
        return jnp.where(index == 0, jnp.concatenate(parts, dim), jnp.concatenate(parts[::-1], dim))
    stacked = jnp.stack(parts)
    order = (index - jnp.arange(peers)) % peers
    return jnp.concatenate([stacked[order[c]] for c in range(peers)], dim)


def swapped(pieces, axis):
    peers = lax.axis_size(axis)
    moves = [[(i, (i + s) % peers) for i in range(peers)] for s in range(peers)]
    return [pieces[0]] + [lax.ppermute(pieces[s], axis, moves[s]) for s in range(1, peers)]


def in_order(parts, axis):
    return by_origin(parts, axis, 3)


def gathered(x, columns, rows):
    nc, nr = lax.axis_size(columns), lax.axis_size(rows)
    c, r = lax.axis_index(columns), lax.axis_index(rows)
    own = x.shape[2] // nc
    odd = r % 2 == 1
    padded = jnp.pad(x, ((0, 0), (0, 0), (2, 2), (0, 0)))
    windows = [lax.dynamic_slice_in_dim(padded, (c + s) % nc * own, own + 4, 2) for s in range(nc)]
    windows = lax.optimization_barrier(windows)
    parts, ones, twos = [windows[0]], [], []
    near, far = pairings(nr)
    for s in range(1, nc):
        parts.append(lax.ppermute(windows[s], columns, [(i, (i + s) % nc) for i in range(nc)]))
    for s in range(nc):
        first, last = windows[s][:, :2], windows[s][:, -2:]
        for to, edge, pairs in ((ones, jnp.where(odd, first, last), near), (twos, jnp.where(odd, last, first), far)):
            moves = [(i * nc + k, j * nc + (k + s) % nc) for i, j in pairs for k in range(nc)]
            to.append(lax.ppermute(edge, (rows, columns), moves))
    one, two = in_order(ones, columns), in_order(twos, columns)
    before, after = beside(one, two, rows)
    return jnp.concatenate([before, in_order(parts, columns), after], 1)


def spread(source, rows, at, sides, info, x3, ef, e3, eb):
    H, Wp, C = source.shape[1:]
    own = Wp - 4

    def step(d):
        x, row = source[d], at + d
        for c in range(3):
            x3[row, :, :, c * C:(c + 1) * C] = x[:, 1 + c:1 + c + own, :]
        for s in range(sides):
            low, high = x[:, 0:3, :], x[:, Wp - 3:Wp, :]
            pick = jnp.where(info[4] == 0, high, low) if sides == 1 else (low, high)[s]
            pick = pick.astype(jnp.float32)
            for l in range(0, C, 128):
                for h in range(H):
                    ef[s, l // 128, pl.ds(h * 8, 3), :] = pick[h, :, l:l + 128]
                for c in range(3):
                    e3[s, 0:H, c * C + l:c * C + l + 128] = ef[s, l // 128, pl.ds(c, H, stride=8), :]
            for b in range(3):
                eb[s, b, row] = e3[s, b:b + H, :].astype(jnp.bfloat16)

    for d in range(rows):
        step(d)


def clear(rows, at, x3, eb):
    for d in range(rows):
        x3[at + d] = jnp.zeros(x3.shape[1:], x3.dtype)
        for s in range(eb.shape[0]):
            for b in range(3):
                eb[s, b, at + d] = jnp.zeros(eb.shape[3:], eb.dtype)


def hidden_sums(d, taps, sides, x3, eb, k1, acc):
    H, own, C = x3.shape[1], x3.shape[2], x3.shape[3] // 3
    H1 = H - 2
    main = 2 * H1 * own
    for a in taps:
        for b in range(3):
            lhs = [x3[d + a:d + a + 2, b:b + H1].reshape(main, 3 * C)]
            lhs += [eb[s, b, d + a:d + a + 2].reshape(2 * H, 3 * C) for s in range(sides)]
            acc += jnp.dot(jnp.concatenate(lhs, 0), k1[a, b].reshape(3 * C, C), preferred_element_type=jnp.float32)
    return acc


def hidden_rows(at, depth, sides, info, own, H, raw, h3):
    C = raw.shape[1]
    H1 = H - 2
    main = 2 * H1 * own
    column = lax.broadcasted_iota(jnp.int32, (own, C), 0)
    none = jnp.zeros((1, C), jnp.float32)

    def step(i):
        q, h = i // H1, i % H1
        ok = jnp.logical_and(depth + q >= 0, depth + q < info[1])
        ok = jnp.logical_and(ok, jnp.logical_or(h > 0, info[2] == 0))
        ok = jnp.logical_and(ok, jnp.logical_or(h < H1 - 1, info[3] == 0))
        row = jnp.where(ok, raw[pl.ds(pl.multiple_of(i * own, 8), own), :], 0.0)
        ends = [raw[pl.ds(main + (s * 2 + q) * H + h, 1), :] for s in range(sides)]
        left = jnp.where(jnp.logical_and(ok, info[4] > 0), ends[0], none)
        right = jnp.where(jnp.logical_and(ok, info[4] < info[5] - 1), ends[sides - 1], none)
        h3[at + q, h, :, 0:C] = jnp.where(column == 0, left, pltpu.roll(row, 1, 0)).astype(jnp.bfloat16)
        h3[at + q, h, :, C:2 * C] = row.astype(jnp.bfloat16)
        h3[at + q, h, :, 2 * C:] = jnp.where(column == own - 1, right, pltpu.roll(row, own - 1, 0)).astype(jnp.bfloat16)

    for i in range(2 * H1):
        step(i)


def feature_rows(h3, k2, bias, o_ref):
    H1, own, C = h3.shape[1], h3.shape[2], h3.shape[3] // 3
    H0 = H1 - 2
    acc = jnp.zeros((2 * H0 * own, C), jnp.float32)
    for a in range(3):
        for b in range(3):
            lhs = h3[a:a + 2, b:b + H0].reshape(2 * H0 * own, 3 * C)
            acc += jnp.dot(lhs, k2[a, b].reshape(3 * C, C), preferred_element_type=jnp.float32)
    o_ref[...] = leaky(acc + bias).astype(jnp.bfloat16).reshape(2, H0, own, C)


def spread(source, rows, at, sides, info, x3, ef, e3, eb):
    H, Wp, C = source.shape[1:]
    own = Wp - 4

    def step(d):
        x, row = source[d], at + d
        for c in range(3):
            x3[row, :, :, c * C:(c + 1) * C] = x[:, 1 + c:1 + c + own, :]
        for s in range(sides):
            low, high = x[:, 0:3, :], x[:, Wp - 3:Wp, :]
            pick = jnp.where(info[4] == 0, high, low) if sides == 1 else (low, high)[s]
            pick = pick.astype(jnp.float32)
            for l in range(0, C, 128):
                for h in range(H):
                    ef[s, l // 128, pl.ds(h * 8, 3), :] = pick[h, :, l:l + 128]
                for c in range(3):
                    e3[s, 0:H, c * C + l:c * C + l + 128] = ef[s, l // 128, pl.ds(c, H, stride=8), :]
            for b in range(3):
                eb[s, b, row] = e3[s, b:b + H, :].astype(jnp.bfloat16)

    for d in range(rows):
        step(d)


def clear(rows, at, x3, eb):
    for d in range(rows):
        x3[at + d] = jnp.zeros(x3.shape[1:], x3.dtype)
        for s in range(eb.shape[0]):
            for b in range(3):
                eb[s, b, at + d] = jnp.zeros(eb.shape[3:], eb.dtype)


def hidden_sums(d, taps, sides, x3, eb, k1, acc):
    H, own, C = x3.shape[1], x3.shape[2], x3.shape[3] // 3
    H1 = H - 2
    main = 2 * H1 * own
    for a in taps:
        for b in range(3):
            lhs = [x3[d + a:d + a + 2, b:b + H1].reshape(main, 3 * C)]
            lhs += [eb[s, b, d + a:d + a + 2].reshape(2 * H, 3 * C) for s in range(sides)]
            acc += jnp.dot(jnp.concatenate(lhs, 0), k1[a, b].reshape(3 * C, C), preferred_element_type=jnp.float32)
    return acc


def hidden_rows(at, depth, sides, info, own, H, raw, h3):
    C = raw.shape[1]
    H1 = H - 2
    main = 2 * H1 * own
    column = lax.broadcasted_iota(jnp.int32, (own, C), 0)
    none = jnp.zeros((1, C), jnp.float32)

    def step(i):
        q, h = i // H1, i % H1
        ok = jnp.logical_and(depth + q >= 0, depth + q < info[1])
        ok = jnp.logical_and(ok, jnp.logical_or(h > 0, info[2] == 0))
        ok = jnp.logical_and(ok, jnp.logical_or(h < H1 - 1, info[3] == 0))
        row = jnp.where(ok, raw[pl.ds(pl.multiple_of(i * own, 8), own), :], 0.0)
        ends = [raw[pl.ds(main + (s * 2 + q) * H + h, 1), :] for s in range(sides)]
        left = jnp.where(jnp.logical_and(ok, info[4] > 0), ends[0], none)
        right = jnp.where(jnp.logical_and(ok, info[4] < info[5] - 1), ends[sides - 1], none)
        h3[at + q, h, :, 0:C] = jnp.where(column == 0, left, pltpu.roll(row, 1, 0)).astype(jnp.bfloat16)
        h3[at + q, h, :, C:2 * C] = row.astype(jnp.bfloat16)
        h3[at + q, h, :, 2 * C:] = jnp.where(column == own - 1, right, pltpu.roll(row, own - 1, 0)).astype(jnp.bfloat16)

    for i in range(2 * H1):
        step(i)


def feature_rows(h3, k2, bias, o_ref):
    H1, own, C = h3.shape[1], h3.shape[2], h3.shape[3] // 3
    H0 = H1 - 2
    acc = jnp.zeros((2 * H0 * own, C), jnp.float32)
    for a in range(3):
        for b in range(3):
            lhs = h3[a:a + 2, b:b + H0].reshape(2 * H0 * own, 3 * C)
            acc += jnp.dot(lhs, k2[a, b].reshape(3 * C, C), preferred_element_type=jnp.float32)
    o_ref[...] = leaky(acc + bias).astype(jnp.bfloat16).reshape(2, H0, own, C)


def places(rows):
    d, h, f = (lax.axis_index(a) for a in ("depth", "height", "filt"))
    nd, nh, nf = (lax.axis_size(a) for a in ("depth", "height", "filt"))
    odd = lax.rem(d, 2)
    end = (d == nd - 1).astype(jnp.int32)
    start = (d == 0).astype(jnp.int32)
    return (d * rows, nd * rows, (h == 0).astype(jnp.int32), (h == nh - 1).astype(jnp.int32), f, nf, odd,
            end * (1 - odd), jnp.where(odd == 1, end, start))


def near_kernel(sides, xc, xn, k1h, b1, k2h, b2, o_ref, keep, k1, k2, x3, ef, e3, eb, h3, raw, sems):
    copies = [pltpu.make_async_copy(k1h.at[a], k1.at[a], sems.at[a]) for a in range(3)]
    copies.append(pltpu.make_async_copy(k2h, k2, sems.at[3]))
    for copy in copies[:2]:
        copy.start()

    D, H, own = xc.shape[0], xc.shape[1], xc.shape[2] - 4
    info = places(D)
    odd = info[6]
    scratch = (x3, ef, e3, eb)
    spread(xc, D, 2 * odd, sides, info, *scratch)
    spread(xn, 2, D * (1 - odd), sides, info, *scratch)

    @pl.when(info[7] > 0)
    def _():
        clear(2, D * (1 - odd), x3, eb)

    for a in range(3):
        copies[a].wait()
        if a < 2:
            copies[a + 2].start()

        @pl.when(odd >= 0)
        def _():
            for t in range(0, D, 2):
                acc = jnp.zeros(raw.shape[1:], jnp.float32) if a == 0 else raw[t // 2]
                raw[t // 2] = hidden_sums(t, [a], sides, x3, eb, k1, acc)
    for t in range(0, D, 2):
        raw[t // 2] = leaky(raw[t // 2] + b1[...])
        hidden_rows(t, info[0] - 1 + 2 * (1 - odd) + t, sides, info, own, H, raw.at[t // 2], h3)
    keep[...] = h3[pl.ds((D - 2) * odd, 2)]
    copies[3].wait()

    @pl.when(odd >= 0)
    def _():
        feature_rows(h3, k2, b2[...], o_ref)


def far_kernel(sides, xc, xf, keep, k1, b1, k2, b2, o_ref, x3, ef, e3, eb, h3, raw):
    D, H, own = xc.shape[0], xc.shape[1], xc.shape[2] - 4
    info = places(D)
    odd = info[6]
    scratch = (x3, ef, e3, eb)
    spread(xc.at[pl.ds((D - 2) * odd, 2)], 2, 2 * (1 - odd), sides, info, *scratch)
    spread(xf, 2, 2 * odd, sides, info, *scratch)

    @pl.when(info[8] > 0)
    def _():
        clear(2, 2 * odd, x3, eb)

    h3[pl.ds(2 * (1 - odd), 2)] = keep[...]

    @pl.when(odd >= 0)
    def _():
        raw[0] = leaky(hidden_sums(0, range(3), sides, x3, eb, k1, jnp.zeros(raw.shape[1:], jnp.float32)) + b1[...])
    hidden_rows(2 * odd, info[0] - 1 + D * odd, sides, info, own, H, raw.at[0], h3)

    @pl.when(odd >= 0)
    def _():
        feature_rows(h3, k2, b2[...], o_ref)


def kernel_call(kernel, name, rows, sides, xc, near, operands):
    D, H, Wp, C = xc.shape
    own = Wp - 4
    weights = jax.ShapeDtypeStruct((3, 3, 3, C, C), jnp.bfloat16)
    out = [jax.ShapeDtypeStruct((2, H - 4, own, C), jnp.bfloat16)]
    scratch = [
        pltpu.VMEM((rows, H, own, 3 * C), jnp.bfloat16),
        pltpu.VMEM((sides, C // 128, H * 8, 128), jnp.float32),
        pltpu.VMEM((sides, 2 * H, 3 * C), jnp.float32),
        pltpu.VMEM((sides, 3, rows, H, 3 * C), jnp.bfloat16),
        pltpu.VMEM((4, H - 2, own, 3 * C), jnp.bfloat16),
        pltpu.VMEM((rows // 2 - 1, 2 * (H - 2) * own + sides * 2 * H, C), jnp.float32),
    ]
    specs = [VMEM] * len(operands)
    if near:
        out += [jax.ShapeDtypeStruct((2, H - 2, own, 3 * C), jnp.bfloat16), weights, weights]
        scratch.append(pltpu.SemaphoreType.DMA((4,)))
        specs[2] = specs[4] = HBM
    hid = (rows - 2) * (H - 2) * own
    return pl.pallas_call(
        functools.partial(kernel, sides),
        out_shape=out,
        in_specs=specs,
        out_specs=[VMEM] * len(out),
        scratch_shapes=scratch,
        compiler_params=pltpu.CompilerParams(vmem_limit_bytes=(43 if near else 24) * 2**20),
        cost_estimate=pl.CostEstimate(flops=2 * 27 * C * C * (hid + 2 * (H - 4) * own), bytes_accessed=2**20, transcendentals=0),
        name=name,
    )(*operands)


def body(volume, kernel_one, bias_one, kernel_two, bias_two):
    b1, b2 = bias_one.reshape(1, -1), bias_two.reshape(1, -1)
    rows, odd = volume.shape[0], lax.axis_index("depth") % 2
    sides = 1 if lax.axis_size("filt") == 2 else 2

    tall = gathered(volume, "filt", "height")
    near, far = exchange(tall[:2], tall[-2:], "depth")
    out_near, keep, k1, k2 = kernel_call(near_kernel, "near", rows + 2, sides, tall, True, (tall, near, kernel_one, b1, kernel_two, b2))
    shard = volume.shape[3]
    def pieces(y):
        f, n = lax.axis_index("filt"), lax.axis_size("filt")
        return [lax.dynamic_slice_in_dim(y, (f + s) % n * shard, shard, 3) for s in range(n)]
    near_pieces, keep = lax.optimization_barrier((pieces(out_near), keep))
    near_parts = swapped(near_pieces, "filt")
    out_far, = kernel_call(far_kernel, "far", 4, sides, tall, False, (tall, far, keep, k1, b1, k2, b2))
    far_parts = swapped(pieces(out_far), "filt")
    out_near, out_far = by_origin(near_parts, "filt", 2), by_origin(far_parts, "filt", 2)
    return jnp.where(odd == 1, jnp.concatenate([out_near, out_far], 0), jnp.concatenate([out_far, out_near], 0))


def solution(mesh):
    in_specs = (P("depth", "height", None, "filt"), P(), P(), P(), P())
    out_specs = P("depth", "height", None, "filt")
    return jax.shard_map(body, mesh=mesh, in_specs=in_specs, out_specs=out_specs, check_vma=False)
```

```python
import functools

import jax
import jax.numpy as jnp
from jax import lax
from jax.experimental import pallas as pl
from jax.experimental.pallas import tpu as pltpu
from jax.sharding import PartitionSpec as P

VMEM = pl.BlockSpec(memory_space=pltpu.VMEM)
HBM = pl.BlockSpec(memory_space=pltpu.HBM)


def leaky(value):
    return jnp.where(value > 0, value, 0.3 * value)


def pairings(peers):
    rounds = []
    for start in (0, 1):
        pairs = [(i, i + 1) for i in range(start, peers - 1, 2)]
        busy = {i for pair in pairs for i in pair}
        rounds.append(pairs + [(j, i) for i, j in pairs] + [(i, i) for i in range(peers) if i not in busy])
    return rounds


def exchange(first, last, axis):
    odd = lax.axis_index(axis) % 2 == 1
    near, far = pairings(lax.axis_size(axis))
    one = lax.ppermute(jnp.where(odd, first, last), axis, near)
    two = lax.ppermute(jnp.where(odd, last, first), axis, far)
    return one, two


def beside(one, two, axis):
    peers, index = lax.axis_size(axis), lax.axis_index(axis)
    odd = index % 2 == 1
    before = jnp.where(odd, one, two)
    after = jnp.where(odd, two, one)
    before = jnp.where(index == 0, jnp.zeros_like(before), before)
    after = jnp.where(index == peers - 1, jnp.zeros_like(after), after)
    return before, after


def by_origin(parts, axis, dim):
    peers, index = lax.axis_size(axis), lax.axis_index(axis)
    if peers == 2:
        return jnp.where(index == 0, jnp.concatenate(parts, dim), jnp.concatenate(parts[::-1], dim))
    stacked = jnp.stack(parts)
    order = (index - jnp.arange(peers)) % peers
    return jnp.concatenate([stacked[order[c]] for c in range(peers)], dim)


def swapped(pieces, axis):
    peers = lax.axis_size(axis)
    moves = [[(i, (i + s) % peers) for i in range(peers)] for s in range(peers)]
    return [pieces[0]] + [lax.ppermute(pieces[s], axis, moves[s]) for s in range(1, peers)]


def in_order(parts, axis):
    return by_origin(parts, axis, 3)


def gathered(x, columns, rows):
    nc, nr = lax.axis_size(columns), lax.axis_size(rows)
    c, r = lax.axis_index(columns), lax.axis_index(rows)
    own = x.shape[2] // nc
    odd = r % 2 == 1
    padded = jnp.pad(x, ((0, 0), (0, 0), (2, 2), (0, 0)))
    windows = [lax.dynamic_slice_in_dim(padded, (c + s) % nc * own, own + 4, 2) for s in range(nc)]
    windows = lax.optimization_barrier(windows)
    parts, ones, twos = [windows[0]], [], []
    near, far = pairings(nr)
    for s in range(1, nc):
        parts.append(lax.ppermute(windows[s], columns, [(i, (i + s) % nc) for i in range(nc)]))
    for s in range(nc):
        first, last = parts[s][:, :2], parts[s][:, -2:]
        ones.append(lax.ppermute(jnp.where(odd, first, last), rows, near))
        twos.append(lax.ppermute(jnp.where(odd, last, first), rows, far))
    one, two = in_order(ones, columns), in_order(twos, columns)
    before, after = beside(one, two, rows)
    return jnp.concatenate([before, in_order(parts, columns), after], 1)


def spread(source, rows, at, sides, info, x3, ef, e3, eb):
    H, Wp, C = source.shape[1:]
    own = Wp - 4

    def step(d):
        x, row = source[d], at + d
        for c in range(3):
            x3[row, :, :, c * C:(c + 1) * C] = x[:, 1 + c:1 + c + own, :]
        for s in range(sides):
            low, high = x[:, 0:3, :], x[:, Wp - 3:Wp, :]
            pick = jnp.where(info[4] == 0, high, low) if sides == 1 else (low, high)[s]
            pick = pick.astype(jnp.float32)
            for l in range(0, C, 128):
                for h in range(H):
                    ef[s, l // 128, pl.ds(h * 8, 3), :] = pick[h, :, l:l + 128]
                for c in range(3):
                    e3[s, 0:H, c * C + l:c * C + l + 128] = ef[s, l // 128, pl.ds(c, H, stride=8), :]
            for b in range(3):
                eb[s, b, row] = e3[s, b:b + H, :].astype(jnp.bfloat16)

    for d in range(rows):
        step(d)


def clear(rows, at, x3, eb):
    for d in range(rows):
        x3[at + d] = jnp.zeros(x3.shape[1:], x3.dtype)
        for s in range(eb.shape[0]):
            for b in range(3):
                eb[s, b, at + d] = jnp.zeros(eb.shape[3:], eb.dtype)


def hidden_sums(d, taps, ends, x3, eb, k1, acc):
    H, own, C = x3.shape[1], x3.shape[2], x3.shape[3] // 3
    main = (H - 2) * own
    for a in taps:
        for b in range(3):
            lhs = [x3[d + a, b:b + H - 2].reshape(main, 3 * C)]
            if ends:
                lhs += [eb[s, b, a:a + ends].reshape(ends * H, 3 * C) for s in range(eb.shape[0])]
            acc += jnp.dot(jnp.concatenate(lhs, 0), k1[a, b].reshape(3 * C, C), preferred_element_type=jnp.float32)
    return acc


def hidden_rows(d, at, depth, sides, info, own, H, raw, ends, h3):
    C = raw.shape[2]
    count = ends.shape[0] // (sides * H)
    column = lax.broadcasted_iota(jnp.int32, (own, C), 0)
    none = jnp.zeros((1, C), jnp.float32)
    inside = jnp.logical_and(depth >= 0, depth < info[1])
    for h in range(H - 2):
        ok = inside
        if h == 0:
            ok = jnp.logical_and(ok, info[2] == 0)
        if h == H - 3:
            ok = jnp.logical_and(ok, info[3] == 0)
        row = jnp.where(ok, raw[d, h * own:(h + 1) * own, :], 0.0)
        edge = [ends[(s * count + d) * H + h:(s * count + d) * H + h + 1, :] for s in range(sides)]
        left = jnp.where(jnp.logical_and(ok, info[4] > 0), edge[0], none)
        right = jnp.where(jnp.logical_and(ok, info[4] < info[5] - 1), edge[sides - 1], none)
        h3[at, h, :, 0:C] = jnp.where(column == 0, left, pltpu.roll(row, 1, 0)).astype(jnp.bfloat16)
        h3[at, h, :, C:2 * C] = row.astype(jnp.bfloat16)
        h3[at, h, :, 2 * C:] = jnp.where(column == own - 1, right, pltpu.roll(row, own - 1, 0)).astype(jnp.bfloat16)


def hidden_part(d, taps, x3, eb, k1, bias, raw, ends):
    main, C = raw.shape[1:]
    size = ends.shape[0] if d == 0 else 0
    if taps[0] == 0:
        acc = jnp.zeros((main + size, C), jnp.float32)
    else:
        acc = jnp.concatenate([raw[d], ends[...]], 0) if size else raw[d]
    acc = hidden_sums(d, taps, raw.shape[0] if size else 0, x3, eb, k1, acc)
    if taps[-1] == 2:
        acc = leaky(acc + bias[...])
    raw[d] = acc[:main]
    if size:
        ends[...] = acc[main:]


def feature_sums(taps, h3, k2, acc):
    H1, own, C = h3.shape[1], h3.shape[2], h3.shape[3] // 3
    H0 = H1 - 2
    for a in taps:
        for b in range(3):
            lhs = h3[a:a + 2, b:b + H0].reshape(2 * H0 * own, 3 * C)
            acc += jnp.dot(lhs, k2[a, b].reshape(3 * C, C), preferred_element_type=jnp.float32)
    return acc


def features(acc, bias, o_ref):
    o_ref[...] = leaky(acc + bias[...]).astype(jnp.bfloat16).reshape(o_ref.shape)


def places(rows):
    d, h, f = (lax.axis_index(a) for a in ("depth", "height", "filt"))
    nd, nh, nf = (lax.axis_size(a) for a in ("depth", "height", "filt"))
    odd = lax.rem(d, 2)
    end = (d == nd - 1).astype(jnp.int32)
    start = (d == 0).astype(jnp.int32)
    return (d * rows, nd * rows, (h == 0).astype(jnp.int32), (h == nh - 1).astype(jnp.int32), f, nf, odd,
            end * (1 - odd), jnp.where(odd == 1, end, start))


def near_kernel(sides, xc, xn, k1h, b1, k2h, b2, o_ref, keep, k1, k2, x3, ef, e3, eb, h3, raw, ends, total, sems):
    copies = [pltpu.make_async_copy(k1h.at[a], k1.at[a], sems.at[a]) for a in range(3)]
    copies += [pltpu.make_async_copy(k2h.at[a], k2.at[a], sems.at[3 + a]) for a in range(3)]
    for copy in copies[:3]:
        copy.start()

    D, H, own = xc.shape[0], xc.shape[1], xc.shape[2] - 4
    info = places(D)
    odd = info[6]
    scratch = (x3, ef, e3, eb)
    spread(xc, D, 2 * odd, sides, info, *scratch)
    spread(xn, 2, D * (1 - odd), sides, info, *scratch)

    @pl.when(info[7] > 0)
    def _():
        clear(2, D * (1 - odd), x3, eb)

    first = info[0] - 1 + 2 * (1 - odd)

    def block(run):
        pl.when(odd >= 0)(run)

    def part(d, taps):
        hidden_part(d, taps, x3, eb, k1, b1, raw, ends)

    def rows(d):
        hidden_rows(d, d, first + d, sides, info, own, H, raw, ends, h3)

    for a in range(3):
        copies[a].wait()
        if a == 0:
            for copy in copies[3:]:
                copy.start()

        @block
        def _():
            for d in range(D):
                part(d, [a])
                if a == 2:
                    rows(d)
    for copy in copies[3:]:
        copy.wait()

    @block
    def _():
        keep[...] = h3[pl.ds((D - 2) * odd, 2)]
        features(feature_sums(range(3), h3, k2, jnp.zeros(total.shape, jnp.float32)), b2, o_ref)


def far_kernel(sides, xc, xf, keep, k1, b1, k2, b2, o_ref, x3, ef, e3, eb, h3, raw, ends, total):
    D, H, own = xc.shape[0], xc.shape[1], xc.shape[2] - 4
    info = places(D)
    odd = info[6]
    scratch = (x3, ef, e3, eb)
    spread(xc.at[pl.ds((D - 2) * odd, 2)], 2, 2 * (1 - odd), sides, info, *scratch)
    spread(xf, 2, 2 * odd, sides, info, *scratch)

    @pl.when(info[8] > 0)
    def _():
        clear(2, 2 * odd, x3, eb)

    h3[pl.ds(2 * (1 - odd), 2)] = keep[...]

    first = info[0] - 1 + D * odd

    @pl.when(odd >= 0)
    def _():
        for d in range(2):
            hidden_part(d, range(3), x3, eb, k1, b1, raw, ends)
        for d in range(2):
            hidden_rows(d, 2 * odd + d, first + d, sides, info, own, H, raw, ends, h3)

    @pl.when(odd >= 0)
    def _():
        features(feature_sums(range(3), h3, k2, jnp.zeros(total.shape, jnp.float32)), b2, o_ref)


def kernel_call(kernel, name, rows, sides, xc, near, operands):
    D, H, Wp, C = xc.shape
    own = Wp - 4
    weights = jax.ShapeDtypeStruct((3, 3, 3, C, C), jnp.bfloat16)
    out = [jax.ShapeDtypeStruct((2, H - 4, own, C), jnp.bfloat16)]
    scratch = [
        pltpu.VMEM((rows, H, own, 3 * C), jnp.bfloat16),
        pltpu.VMEM((sides, C // 128, H * 8, 128), jnp.float32),
        pltpu.VMEM((sides, 2 * H, 3 * C), jnp.float32),
        pltpu.VMEM((sides, 3, rows, H, 3 * C), jnp.bfloat16),
        pltpu.VMEM((4, H - 2, own, 3 * C), jnp.bfloat16),
        pltpu.VMEM((rows - 2, (H - 2) * own, C), jnp.float32),
        pltpu.VMEM((sides * (rows - 2) * H, C), jnp.float32),
        pltpu.VMEM((2 * (H - 4) * own, C), jnp.float32),
    ]
    specs = [VMEM] * len(operands)
    if near:
        out += [jax.ShapeDtypeStruct((2, H - 2, own, 3 * C), jnp.bfloat16), weights, weights]
        scratch.append(pltpu.SemaphoreType.DMA((6,)))
        specs[2] = specs[4] = HBM
    hid = (rows - 2) * (H - 2) * own
    return pl.pallas_call(
        functools.partial(kernel, sides),
        out_shape=out,
        in_specs=specs,
        out_specs=[VMEM] * len(out),
        scratch_shapes=scratch,
        compiler_params=pltpu.CompilerParams(vmem_limit_bytes=(43 if near else 24) * 2**20),
        cost_estimate=pl.CostEstimate(flops=2 * 27 * C * C * (hid + 2 * (H - 4) * own), bytes_accessed=2**20, transcendentals=0),
        name=name,
    )(*operands)


def body(volume, kernel_one, bias_one, kernel_two, bias_two):
    b1, b2 = bias_one.reshape(1, -1), bias_two.reshape(1, -1)
    rows, odd = volume.shape[0], lax.axis_index("depth") % 2
    sides = 1 if lax.axis_size("filt") == 2 else 2

    tall = gathered(volume, "filt", "height")
    near, far = exchange(tall[:2], tall[-2:], "depth")
    out_near, keep, k1, k2 = kernel_call(near_kernel, "near", rows + 2, sides, tall, True, (tall, near, kernel_one, b1, kernel_two, b2))
    shard = volume.shape[3]
    def pieces(y):
        f, n = lax.axis_index("filt"), lax.axis_size("filt")
        return [lax.dynamic_slice_in_dim(y, (f + s) % n * shard, shard, 3) for s in range(n)]
    out_far, = kernel_call(far_kernel, "far", 4, sides, tall, False, (tall, far, keep, k1, b1, k2, b2))
    out = jnp.where(odd == 1, jnp.concatenate([out_near, out_far], 0), jnp.concatenate([out_far, out_near], 0))
    return by_origin(swapped(pieces(out), "filt"), "filt", 2)


def solution(mesh):
    in_specs = (P("depth", "height", None, "filt"), P(), P(), P(), P())
    out_specs = P("depth", "height", None, "filt")
    return jax.shard_map(body, mesh=mesh, in_specs=in_specs, out_specs=out_specs, check_vma=False)
```

```python
import functools

import jax
import jax.numpy as jnp
from jax import lax
from jax.experimental import pallas as pl
from jax.experimental.pallas import tpu as pltpu
from jax.sharding import PartitionSpec as P

VMEM = pl.BlockSpec(memory_space=pltpu.VMEM)
HBM = pl.BlockSpec(memory_space=pltpu.HBM)


def leaky(value):
    return jnp.where(value > 0, value, 0.3 * value)


def pairings(peers):
    rounds = []
    for start in (0, 1):
        pairs = [(i, i + 1) for i in range(start, peers - 1, 2)]
        busy = {i for pair in pairs for i in pair}
        rounds.append(pairs + [(j, i) for i, j in pairs] + [(i, i) for i in range(peers) if i not in busy])
    return rounds


def exchange(first, last, axis):
    odd = lax.axis_index(axis) % 2 == 1
    near, far = pairings(lax.axis_size(axis))
    one = lax.ppermute(jnp.where(odd, first, last), axis, near)
    two = lax.ppermute(jnp.where(odd, last, first), axis, far)
    return one, two


def beside(one, two, axis):
    peers, index = lax.axis_size(axis), lax.axis_index(axis)
    odd = index % 2 == 1
    before = jnp.where(odd, one, two)
    after = jnp.where(odd, two, one)
    before = jnp.where(index == 0, jnp.zeros_like(before), before)
    after = jnp.where(index == peers - 1, jnp.zeros_like(after), after)
    return before, after


def by_origin(parts, axis, dim):
    peers, index = lax.axis_size(axis), lax.axis_index(axis)
    if peers == 2:
        return jnp.where(index == 0, jnp.concatenate(parts, dim), jnp.concatenate(parts[::-1], dim))
    stacked = jnp.stack(parts)
    order = (index - jnp.arange(peers)) % peers
    return jnp.concatenate([stacked[order[c]] for c in range(peers)], dim)


def swapped(pieces, axis):
    peers = lax.axis_size(axis)
    moves = [[(i, (i + s) % peers) for i in range(peers)] for s in range(peers)]
    return [pieces[0]] + [lax.ppermute(pieces[s], axis, moves[s]) for s in range(1, peers)]


def in_order(parts, axis):
    return by_origin(parts, axis, 3)


def gathered(x, columns, rows, extra):
    nc, nr = lax.axis_size(columns), lax.axis_size(rows)
    c, r = lax.axis_index(columns), lax.axis_index(rows)
    own = x.shape[2] // nc
    odd = r % 2 == 1
    def halves(s, x):
        padded = jnp.pad(x, ((0, 0), (0, 0), (2, 2), (0, 0)))
        w = lax.dynamic_slice_in_dim(padded, (c + s) % nc * own, own + 4, 2)
        return jnp.where(odd, w[:, :2], w[:, -2:]), jnp.where(odd, w[:, -2:], w[:, :2])

    sent = lax.optimization_barrier([halves(s, x) for s in range(1, nc)])
    again, extra = lax.optimization_barrier((x, extra))
    kept = halves(0, again)
    got = []
    for r in range(2):
        parts = [kept[r]] + [lax.ppermute(sent[s - 1][r], columns, [(i, (i + s) % nc) for i in range(nc)]) for s in range(1, nc)]
        got.append(in_order(parts, columns))
    near, far = pairings(nr)
    one = lax.ppermute(got[0], rows, near)
    two = lax.ppermute(got[1], rows, far)
    two, one = lax.optimization_barrier((two, one))
    before, after = beside(one, two, rows)
    whole = jnp.where(odd, jnp.concatenate(got, 1), jnp.concatenate(got[::-1], 1))
    return jnp.concatenate([before, whole, after], 1), extra


def spread(source, rows, at, sides, info, x3, ef, e3, eb):
    H, Wp, C = source.shape[1:]
    own = Wp - 4

    def step(d):
        x, row = source[d], at + d
        for c in range(3):
            x3[row, :, :, c * C:(c + 1) * C] = x[:, 1 + c:1 + c + own, :]
        for s in range(sides):
            low, high = x[:, 0:3, :], x[:, Wp - 3:Wp, :]
            pick = jnp.where(info[4] == 0, high, low) if sides == 1 else (low, high)[s]
            pick = pick.astype(jnp.float32)
            for l in range(0, C, 128):
                for h in range(H):
                    ef[s, l // 128, pl.ds(h * 8, 3), :] = pick[h, :, l:l + 128]
                for c in range(3):
                    e3[s, 0:H, c * C + l:c * C + l + 128] = ef[s, l // 128, pl.ds(c, H, stride=8), :]
            for b in range(3):
                eb[s, b, row] = e3[s, b:b + H, :].astype(jnp.bfloat16)

    for d in range(rows):
        step(d)


def clear(rows, at, x3, eb):
    for d in range(rows):
        x3[at + d] = jnp.zeros(x3.shape[1:], x3.dtype)
        for s in range(eb.shape[0]):
            for b in range(3):
                eb[s, b, at + d] = jnp.zeros(eb.shape[3:], eb.dtype)


def hidden_sums(d, taps, ends, x3, eb, k1, acc):
    H, own, C = x3.shape[1], x3.shape[2], x3.shape[3] // 3
    main = (H - 2) * own
    for a in taps:
        for b in range(3):
            lhs = [x3[d + a, b:b + H - 2].reshape(main, 3 * C)]
            if ends:
                lhs += [eb[s, b, a:a + ends].reshape(ends * H, 3 * C) for s in range(eb.shape[0])]
            acc += jnp.dot(jnp.concatenate(lhs, 0), k1[a, b].reshape(3 * C, C), preferred_element_type=jnp.float32)
    return acc


def hidden_rows(d, at, depth, sides, info, own, H, raw, ends, h3):
    C = raw.shape[2]
    count = ends.shape[0] // (sides * H)
    column = lax.broadcasted_iota(jnp.int32, (own, C), 0)
    none = jnp.zeros((1, C), jnp.float32)
    inside = jnp.logical_and(depth >= 0, depth < info[1])
    for h in range(H - 2):
        ok = inside
        if h == 0:
            ok = jnp.logical_and(ok, info[2] == 0)
        if h == H - 3:
            ok = jnp.logical_and(ok, info[3] == 0)
        row = jnp.where(ok, raw[d, h * own:(h + 1) * own, :], 0.0)
        edge = [ends[(s * count + d) * H + h:(s * count + d) * H + h + 1, :] for s in range(sides)]
        left = jnp.where(jnp.logical_and(ok, info[4] > 0), edge[0], none)
        right = jnp.where(jnp.logical_and(ok, info[4] < info[5] - 1), edge[sides - 1], none)
        h3[at, h, :, 0:C] = jnp.where(column == 0, left, pltpu.roll(row, 1, 0)).astype(jnp.bfloat16)
        h3[at, h, :, C:2 * C] = row.astype(jnp.bfloat16)
        h3[at, h, :, 2 * C:] = jnp.where(column == own - 1, right, pltpu.roll(row, own - 1, 0)).astype(jnp.bfloat16)


def hidden_part(d, taps, x3, eb, k1, bias, raw, ends):
    main, C = raw.shape[1:]
    size = ends.shape[0] if d == 0 else 0
    if taps[0] == 0:
        acc = jnp.zeros((main + size, C), jnp.float32)
    else:
        acc = jnp.concatenate([raw[d], ends[...]], 0) if size else raw[d]
    acc = hidden_sums(d, taps, raw.shape[0] if size else 0, x3, eb, k1, acc)
    if taps[-1] == 2:
        acc = leaky(acc + bias[...])
    raw[d] = acc[:main]
    if size:
        ends[...] = acc[main:]


def feature_sums(taps, h3, k2, acc):
    H1, own, C = h3.shape[1], h3.shape[2], h3.shape[3] // 3
    H0 = H1 - 2
    for a in taps:
        for b in range(3):
            lhs = h3[a:a + 2, b:b + H0].reshape(2 * H0 * own, 3 * C)
            acc += jnp.dot(lhs, k2[a, b].reshape(3 * C, C), preferred_element_type=jnp.float32)
    return acc


def features(acc, bias, o_ref):
    o_ref[...] = leaky(acc + bias[...]).astype(jnp.bfloat16).reshape(o_ref.shape)


def places(rows):
    d, h, f = (lax.axis_index(a) for a in ("depth", "height", "filt"))
    nd, nh, nf = (lax.axis_size(a) for a in ("depth", "height", "filt"))
    odd = lax.rem(d, 2)
    end = (d == nd - 1).astype(jnp.int32)
    start = (d == 0).astype(jnp.int32)
    return (d * rows, nd * rows, (h == 0).astype(jnp.int32), (h == nh - 1).astype(jnp.int32), f, nf, odd,
            end * (1 - odd), jnp.where(odd == 1, end, start))


def near_kernel(sides, xc, xn, k0, k1h, b1, k2h, b2, o_ref, keep, k1, k2, x3, ef, e3, eb, h3, raw, ends, total, sems):
    copies = [pltpu.make_async_copy(k1h.at[a], k1.at[a], sems.at[a]) for a in range(3)]
    copies += [pltpu.make_async_copy(k2h.at[a], k2.at[a], sems.at[3 + a]) for a in range(3)]
    for copy in copies[1:3]:
        copy.start()
    D, H, own = xc.shape[0], xc.shape[1], xc.shape[2] - 4
    info = places(D)
    odd = info[6]
    scratch = (x3, ef, e3, eb)
    spread(xc, D, 2 * odd, sides, info, *scratch)
    spread(xn, 2, D * (1 - odd), sides, info, *scratch)

    @pl.when(info[7] > 0)
    def _():
        clear(2, D * (1 - odd), x3, eb)

    first = info[0] - 1 + 2 * (1 - odd)

    def block(run):
        pl.when(odd >= 0)(run)

    def part(d, taps):
        hidden_part(d, taps, x3, eb, k1 if taps[0] else k0, b1, raw, ends)

    def rows(d):
        hidden_rows(d, d, first + d, sides, info, own, H, raw, ends, h3)

    for a in range(3):
        if a > 0:
            copies[a].wait()
        if a == 1:
            for copy in copies[3:] + copies[:1]:
                copy.start()

        @block
        def _():
            for d in range(D):
                part(d, [a])
                if a == 2:
                    rows(d)
    for copy in copies[3:] + copies[:1]:
        copy.wait()

    @block
    def _():
        keep[...] = h3[pl.ds((D - 2) * odd, 2)]
        features(feature_sums(range(3), h3, k2, jnp.zeros(total.shape, jnp.float32)), b2, o_ref)


def far_kernel(sides, xc, xf, keep, k1, b1, k2, b2, o_ref, x3, ef, e3, eb, h3, raw, ends, total):
    D, H, own = xc.shape[0], xc.shape[1], xc.shape[2] - 4
    info = places(D)
    odd = info[6]
    scratch = (x3, ef, e3, eb)
    spread(xc.at[pl.ds((D - 2) * odd, 2)], 2, 2 * (1 - odd), sides, info, *scratch)
    spread(xf, 2, 2 * odd, sides, info, *scratch)

    @pl.when(info[8] > 0)
    def _():
        clear(2, 2 * odd, x3, eb)

    h3[pl.ds(2 * (1 - odd), 2)] = keep[...]

    first = info[0] - 1 + D * odd

    @pl.when(odd >= 0)
    def _():
        for d in range(2):
            hidden_part(d, range(3), x3, eb, k1, b1, raw, ends)
        for d in range(2):
            hidden_rows(d, 2 * odd + d, first + d, sides, info, own, H, raw, ends, h3)

    @pl.when(odd >= 0)
    def _():
        features(feature_sums(range(3), h3, k2, jnp.zeros(total.shape, jnp.float32)), b2, o_ref)


def kernel_call(kernel, name, rows, sides, xc, near, operands):
    D, H, Wp, C = xc.shape
    own = Wp - 4
    weights = jax.ShapeDtypeStruct((3, 3, 3, C, C), jnp.bfloat16)
    out = [jax.ShapeDtypeStruct((2, H - 4, own, C), jnp.bfloat16)]
    scratch = [
        pltpu.VMEM((rows, H, own, 3 * C), jnp.bfloat16),
        pltpu.VMEM((sides, C // 128, H * 8, 128), jnp.float32),
        pltpu.VMEM((sides, 2 * H, 3 * C), jnp.float32),
        pltpu.VMEM((sides, 3, rows, H, 3 * C), jnp.bfloat16),
        pltpu.VMEM((4, H - 2, own, 3 * C), jnp.bfloat16),
        pltpu.VMEM((rows - 2, (H - 2) * own, C), jnp.float32),
        pltpu.VMEM((sides * (rows - 2) * H, C), jnp.float32),
        pltpu.VMEM((2 * (H - 4) * own, C), jnp.float32),
    ]
    specs = [VMEM] * len(operands)
    if near:
        out += [jax.ShapeDtypeStruct((2, H - 2, own, 3 * C), jnp.bfloat16), weights, weights]
        scratch.append(pltpu.SemaphoreType.DMA((6,)))
        specs[3] = specs[5] = HBM
    hid = (rows - 2) * (H - 2) * own
    return pl.pallas_call(
        functools.partial(kernel, sides),
        out_shape=out,
        in_specs=specs,
        out_specs=[VMEM] * len(out),
        scratch_shapes=scratch,
        compiler_params=pltpu.CompilerParams(vmem_limit_bytes=(43 if near else 24) * 2**20),
        cost_estimate=pl.CostEstimate(flops=2 * 27 * C * C * (hid + 2 * (H - 4) * own), bytes_accessed=2**20, transcendentals=0),
        name=name,
    )(*operands)


def body(volume, kernel_one, bias_one, kernel_two, bias_two):
    b1, b2 = bias_one.reshape(1, -1), bias_two.reshape(1, -1)
    rows, odd = volume.shape[0], lax.axis_index("depth") % 2
    sides = 1 if lax.axis_size("filt") == 2 else 2

    tall, k0 = gathered(volume, "filt", "height", kernel_one[:1])
    near, far = exchange(tall[:2], tall[-2:], "depth")
    out_near, keep, k1, k2 = kernel_call(near_kernel, "near", rows + 2, sides, tall, True, (tall, near, k0, kernel_one, b1, kernel_two, b2))
    shard = volume.shape[3]
    def pieces(y):
        f, n = lax.axis_index("filt"), lax.axis_size("filt")
        return [lax.dynamic_slice_in_dim(y, (f + s) % n * shard, shard, 3) for s in range(n)]
    out_far, = kernel_call(far_kernel, "far", 4, sides, tall, False, (tall, far, keep, k1, b1, k2, b2))
    out = jnp.where(odd == 1, jnp.concatenate([out_near, out_far], 0), jnp.concatenate([out_far, out_near], 0))
    return by_origin(swapped(pieces(out), "filt"), "filt", 2)


def solution(mesh):
    in_specs = (P("depth", "height", None, "filt"), P(), P(), P(), P())
    out_specs = P("depth", "height", None, "filt")
    return jax.shard_map(body, mesh=mesh, in_specs=in_specs, out_specs=out_specs, check_vma=False)
```

```python
import functools

import jax
import jax.numpy as jnp
from jax import lax
from jax.experimental import pallas as pl
from jax.experimental.pallas import tpu as pltpu
from jax.sharding import PartitionSpec as P

VMEM = pl.BlockSpec(memory_space=pltpu.VMEM)
HBM = pl.BlockSpec(memory_space=pltpu.HBM)


def leaky(value):
    return jnp.where(value > 0, value, 0.3 * value)


def pairings(peers):
    rounds = []
    for start in (0, 1):
        pairs = [(i, i + 1) for i in range(start, peers - 1, 2)]
        busy = {i for pair in pairs for i in pair}
        rounds.append(pairs + [(j, i) for i, j in pairs] + [(i, i) for i in range(peers) if i not in busy])
    return rounds


def exchange(first, last, axis):
    odd = lax.axis_index(axis) % 2 == 1
    near, far = pairings(lax.axis_size(axis))
    one = lax.ppermute(jnp.where(odd, first, last), axis, near)
    two = lax.ppermute(jnp.where(odd, last, first), axis, far)
    return one, two


def beside(one, two, axis):
    peers, index = lax.axis_size(axis), lax.axis_index(axis)
    odd = index % 2 == 1
    before = jnp.where(odd, one, two)
    after = jnp.where(odd, two, one)
    before = jnp.where(index == 0, jnp.zeros_like(before), before)
    after = jnp.where(index == peers - 1, jnp.zeros_like(after), after)
    return before, after


def by_origin(parts, axis, dim):
    peers, index = lax.axis_size(axis), lax.axis_index(axis)
    if peers == 2:
        return jnp.where(index == 0, jnp.concatenate(parts, dim), jnp.concatenate(parts[::-1], dim))
    stacked = jnp.stack(parts)
    order = (index - jnp.arange(peers)) % peers
    return jnp.concatenate([stacked[order[c]] for c in range(peers)], dim)


def swapped(pieces, axis):
    peers = lax.axis_size(axis)
    moves = [[(i, (i + s) % peers) for i in range(peers)] for s in range(peers)]
    return [pieces[0]] + [lax.ppermute(pieces[s], axis, moves[s]) for s in range(1, peers)]


def in_order(parts, axis):
    return by_origin(parts, axis, 3)


def gathered(x, columns, rows, extra):
    nc, nr = lax.axis_size(columns), lax.axis_size(rows)
    c, r = lax.axis_index(columns), lax.axis_index(rows)
    own, shard = x.shape[2] // nc, x.shape[3]
    odd = r % 2 == 1

    def window(s, x):
        block = (c + s) % nc
        if nc == 2:
            return jnp.where(block == 0, x[:, :, :own + 8], x[:, :, own - 8:])
        padded = jnp.pad(x, ((0, 0), (0, 0), (2, 2), (0, 0)))
        return lax.dynamic_slice_in_dim(padded, block * own, own + 4, 2)

    def halves(s, near):
        block = (c + s) % nc
        if nc == 2:
            main = jnp.where(block == 0, near[:, :, :own], near[:, :, 8:])
            ends = jnp.where(block == 0, near[:, :, own:own + 2], near[:, :, 6:8])
        else:
            main, ends = near[:, :, 2:-2], jnp.concatenate([near[:, :, :2], near[:, :, -2:]], 2)

        def flat(rows):
            return jnp.concatenate([main[:, rows].reshape(-1, shard), ends[:, rows].reshape(-1, shard)], 0)
        first, last = flat(slice(0, 2)), flat(slice(2, 4))
        return jnp.where(odd, first, last), jnp.where(odd, last, first)

    windows = lax.optimization_barrier([window(s, x) for s in range(1, nc)])
    sent = [halves(s, windows[s - 1]) for s in range(1, nc)]
    again, extra = lax.optimization_barrier((x, extra))
    kept = halves(0, lax.optimization_barrier(window(0, again)))
    got = []
    for r_ in range(2):
        parts = [kept[r_]] + [lax.ppermute(sent[s - 1][r_], columns, [(i, (i + s) % nc) for i in range(nc)]) for s in range(1, nc)]
        got.append(by_origin(parts, columns, 1))
    near, far = pairings(nr)
    one = lax.ppermute(got[0], rows, near)
    two = lax.ppermute(got[1], rows, far)
    before, after = beside(one, two, rows)
    inner = jnp.where(odd, jnp.stack(got), jnp.stack(got[::-1]))
    return jnp.concatenate([before[None], inner, after[None]], 0), extra


def depth_rows(pairs, first, depth, own):
    ends = pairs.shape[1] // depth // 2 - own
    at = 2 * first * own, 2 * (depth * own + first * ends)
    main = pairs[:, at[0]:at[0] + 4 * own].reshape(-1, pairs.shape[2])
    return jnp.concatenate([main, pairs[:, at[1]:at[1] + 4 * ends].reshape(-1, pairs.shape[2])], 0)


def from_pairs(ref, own, depth):
    def row(d):
        pairs, C = ref.shape[0], ref.shape[2]
        ends = ref.shape[1] // depth // 2 - own
        main = [ref[p, 2 * d * own:2 * (d + 1) * own, :].reshape(2, own, C) for p in range(pairs)]
        tail = [ref[p, 2 * depth * own:, :].astype(jnp.float32)[2 * d * ends:2 * (d + 1) * ends] for p in range(pairs)]
        return jnp.concatenate(main, 0), tail
    return row


def from_rows(ref, own, pairs):
    def row(d):
        C = ref.shape[1]
        ends = ref.shape[0] // pairs // 4 - own
        main = [ref[(2 * p + d) * 2 * own:(2 * p + d + 1) * 2 * own, :].reshape(2, own, C) for p in range(pairs)]
        tail = ref[4 * pairs * own:, :].astype(jnp.float32)
        return jnp.concatenate(main, 0), [tail[(2 * p + d) * 2 * ends:(2 * p + d + 1) * 2 * ends] for p in range(pairs)]
    return row


def either(odd, one, two):
    return jax.tree.map(lambda a, b: jnp.where(odd == 1, a, b), one, two)


def spread(source, rows, at, sides, info, x3, ef, et, eb):
    H, own, C = x3.shape[1], x3.shape[2], x3.shape[3] // 3
    column = lax.broadcasted_iota(jnp.int32, (own, C), 0)
    f, none = info[4], jnp.zeros((H, C), jnp.float32)
    ends = 2 * sides
    for d in range(rows):
        x, tail = source(d)
        row = at + d
        picks = [x[:, own - 1:own, :], x[:, 0:1, :]]
        if sides == 1:
            picks = [jnp.where(f == 0, picks[0], picks[1])]
        edge = [[] for _ in range(ends + len(picks))]
        for l in range(0, C, 128):
            for p, part in enumerate(tail):
                et[l // 128, 2 * p * ends:2 * (p + 1) * ends, :] = part[:, l:l + 128]
            for e in range(ends):
                edge[e].append(et[l // 128, pl.ds(e, H, stride=ends), :])
            for k, pick in enumerate(picks):
                for h in range(H):
                    ef[k, l // 128, h * 8:h * 8 + 1, :] = pick[h, :, l:l + 128].astype(jnp.float32)
                edge[ends + k].append(ef[k, l // 128, pl.ds(0, H, stride=8), :])
        edge = [jnp.concatenate(e, 1) for e in edge]
        if sides == 1:
            e0, e1, inner = edge
            left, right = jnp.where(f == 0, none, e1), jnp.where(f == 0, e0, none)
            taps = [[jnp.where(f == 0, inner, e0), jnp.where(f == 0, e0, e1), jnp.where(f == 0, e1, inner)]]
        else:
            l0, l1, r0, r1, last, first = edge
            left, right = l1, r0
            taps = [[l0, l1, first], [last, r0, r1]]
        for s in range(sides):
            wide = jnp.concatenate(taps[s], 1)
            for b in range(3):
                moved = wide if b == 0 else pltpu.roll(wide, H - b, 0)
                eb[s, b, row] = moved.astype(jnp.bfloat16)
        for h in range(H):
            line = x[h].astype(jnp.float32)
            x3[row, h, :, 0:C] = jnp.where(column == 0, left[h:h + 1], pltpu.roll(line, 1, 0)).astype(jnp.bfloat16)
            x3[row, h, :, C:2 * C] = x[h]
            x3[row, h, :, 2 * C:] = jnp.where(column == own - 1, right[h:h + 1], pltpu.roll(line, own - 1, 0)).astype(jnp.bfloat16)


def clear(rows, at, x3, eb):
    for d in range(rows):
        x3[at + d] = jnp.zeros(x3.shape[1:], x3.dtype)
        for s in range(eb.shape[0]):
            for b in range(3):
                eb[s, b, at + d] = jnp.zeros(eb.shape[3:], eb.dtype)


def hidden_sums(d, taps, ends, x3, eb, k1, acc):
    H, own, C = x3.shape[1], x3.shape[2], x3.shape[3] // 3
    main = (H - 2) * own
    for a in taps:
        for b in range(3):
            lhs = [x3[d + a, b:b + H - 2].reshape(main, 3 * C)]
            if ends:
                lhs += [eb[s, b, a:a + ends].reshape(ends * H, 3 * C) for s in range(eb.shape[0])]
            acc += jnp.dot(jnp.concatenate(lhs, 0), k1[a, b].reshape(3 * C, C), preferred_element_type=jnp.float32)
    return acc


def hidden_rows(d, at, depth, sides, info, own, H, raw, ends, h3):
    C = raw.shape[2]
    count = ends.shape[0] // (sides * H)
    column = lax.broadcasted_iota(jnp.int32, (own, C), 0)
    none = jnp.zeros((1, C), jnp.float32)
    inside = jnp.logical_and(depth >= 0, depth < info[1])
    for h in range(H - 2):
        ok = inside
        if h == 0:
            ok = jnp.logical_and(ok, info[2] == 0)
        if h == H - 3:
            ok = jnp.logical_and(ok, info[3] == 0)
        row = jnp.where(ok, raw[d, h * own:(h + 1) * own, :], 0.0)
        edge = [ends[(s * count + d) * H + h:(s * count + d) * H + h + 1, :] for s in range(sides)]
        left = jnp.where(jnp.logical_and(ok, info[4] > 0), edge[0], none)
        right = jnp.where(jnp.logical_and(ok, info[4] < info[5] - 1), edge[sides - 1], none)
        h3[at, h, :, 0:C] = jnp.where(column == 0, left, pltpu.roll(row, 1, 0)).astype(jnp.bfloat16)
        h3[at, h, :, C:2 * C] = row.astype(jnp.bfloat16)
        h3[at, h, :, 2 * C:] = jnp.where(column == own - 1, right, pltpu.roll(row, own - 1, 0)).astype(jnp.bfloat16)


def hidden_part(d, taps, x3, eb, k1, bias, raw, ends):
    main, C = raw.shape[1:]
    size = ends.shape[0] if d == 0 else 0
    if taps[0] == 0:
        acc = jnp.zeros((main + size, C), jnp.float32)
    else:
        acc = jnp.concatenate([raw[d], ends[...]], 0) if size else raw[d]
    acc = hidden_sums(d, taps, raw.shape[0] if size else 0, x3, eb, k1, acc)
    if taps[-1] == 2:
        acc = leaky(acc + bias[...])
    raw[d] = acc[:main]
    if size:
        ends[...] = acc[main:]


def feature_sums(taps, h3, k2, acc):
    H1, own, C = h3.shape[1], h3.shape[2], h3.shape[3] // 3
    H0 = H1 - 2
    for a in taps:
        for b in range(3):
            lhs = h3[a:a + 2, b:b + H0].reshape(2 * H0 * own, 3 * C)
            acc += jnp.dot(lhs, k2[a, b].reshape(3 * C, C), preferred_element_type=jnp.float32)
    return acc


def features(acc, bias, o_ref):
    o_ref[...] = leaky(acc + bias[...]).astype(jnp.bfloat16).reshape(o_ref.shape)


def places(rows):
    d, h, f = (lax.axis_index(a) for a in ("depth", "height", "filt"))
    nd, nh, nf = (lax.axis_size(a) for a in ("depth", "height", "filt"))
    odd = lax.rem(d, 2)
    end = (d == nd - 1).astype(jnp.int32)
    start = (d == 0).astype(jnp.int32)
    return (d * rows, nd * rows, (h == 0).astype(jnp.int32), (h == nh - 1).astype(jnp.int32), f, nf, odd,
            end * (1 - odd), jnp.where(odd == 1, end, start))


def near_kernel(sides, depth, xc, xn, k0, k1h, b1, k2h, b2, o_ref, keep, k1, k2, x3, ef, et, eb, h3, raw, ends, total, sems):
    copies = [pltpu.make_async_copy(k1h.at[a], k1.at[a], sems.at[a]) for a in range(3)]
    copies += [pltpu.make_async_copy(k2h.at[a], k2.at[a], sems.at[3 + a]) for a in range(3)]
    for copy in copies[1:3]:
        copy.start()
    D, H, own = depth, x3.shape[1], x3.shape[2]
    info = places(D)
    odd = info[6]
    scratch = (x3, ef, et, eb)
    spread(from_pairs(xc, own, D), D, 2 * odd, sides, info, *scratch)
    spread(from_rows(xn, own, H // 2), 2, D * (1 - odd), sides, info, *scratch)

    @pl.when(info[7] > 0)
    def _():
        clear(2, D * (1 - odd), x3, eb)

    first = info[0] - 1 + 2 * (1 - odd)

    def block(run):
        pl.when(odd >= 0)(run)

    def part(d, taps):
        hidden_part(d, taps, x3, eb, k1 if taps[0] else k0, b1, raw, ends)

    def rows(d):
        hidden_rows(d, d, first + d, sides, info, own, H, raw, ends, h3)

    for a in range(3):
        if a > 0:
            copies[a].wait()
        if a == 1:
            for copy in copies[3:] + copies[:1]:
                copy.start()

        @block
        def _():
            for d in range(D):
                part(d, [a])
                if a == 2:
                    rows(d)
    for copy in copies[3:] + copies[:1]:
        copy.wait()

    @block
    def _():
        keep[...] = h3[pl.ds((D - 2) * odd, 2)]
        features(feature_sums(range(3), h3, k2, jnp.zeros(total.shape, jnp.float32)), b2, o_ref)


def far_kernel(sides, depth, xc, xf, keep, k1, b1, k2, b2, o_ref, x3, ef, et, eb, h3, raw, ends, total):
    D, H, own = depth, x3.shape[1], x3.shape[2]
    info = places(D)
    odd = info[6]
    scratch = (x3, ef, et, eb)
    tall = from_pairs(xc, own, D)
    spread(lambda d: either(odd, tall(D - 2 + d), tall(d)), 2, 2 * (1 - odd), sides, info, *scratch)
    spread(from_rows(xf, own, H // 2), 2, 2 * odd, sides, info, *scratch)

    @pl.when(info[8] > 0)
    def _():
        clear(2, 2 * odd, x3, eb)

    h3[pl.ds(2 * (1 - odd), 2)] = keep[...]

    first = info[0] - 1 + D * odd

    @pl.when(odd >= 0)
    def _():
        for d in range(2):
            hidden_part(d, range(3), x3, eb, k1, b1, raw, ends)
        for d in range(2):
            hidden_rows(d, 2 * odd + d, first + d, sides, info, own, H, raw, ends, h3)

    @pl.when(odd >= 0)
    def _():
        features(feature_sums(range(3), h3, k2, jnp.zeros(total.shape, jnp.float32)), b2, o_ref)


def kernel_call(kernel, name, rows, sides, shape, near, operands):
    D, H, own, C = shape
    weights = jax.ShapeDtypeStruct((3, 3, 3, C, C), jnp.bfloat16)
    out = [jax.ShapeDtypeStruct((2, H - 4, own, C), jnp.bfloat16)]
    scratch = [
        pltpu.VMEM((rows, H, own, 3 * C), jnp.bfloat16),
        pltpu.VMEM((sides, C // 128, H * 8, 128), jnp.float32),
        pltpu.VMEM((C // 128, 2 * sides * H, 128), jnp.float32),
        pltpu.VMEM((sides, 3, rows, H, 3 * C), jnp.bfloat16),
        pltpu.VMEM((4, H - 2, own, 3 * C), jnp.bfloat16),
        pltpu.VMEM((rows - 2, (H - 2) * own, C), jnp.float32),
        pltpu.VMEM((sides * (rows - 2) * H, C), jnp.float32),
        pltpu.VMEM((2 * (H - 4) * own, C), jnp.float32),
    ]
    specs = [VMEM] * len(operands)
    if near:
        out += [jax.ShapeDtypeStruct((2, H - 2, own, 3 * C), jnp.bfloat16), weights, weights]
        scratch.append(pltpu.SemaphoreType.DMA((6,)))
        specs[3] = specs[5] = HBM
    hid = (rows - 2) * (H - 2) * own
    return pl.pallas_call(
        functools.partial(kernel, sides, D),
        out_shape=out,
        in_specs=specs,
        out_specs=[VMEM] * len(out),
        scratch_shapes=scratch,
        compiler_params=pltpu.CompilerParams(vmem_limit_bytes=(43 if near else 24) * 2**20),
        cost_estimate=pl.CostEstimate(flops=2 * 27 * C * C * (hid + 2 * (H - 4) * own), bytes_accessed=2**20, transcendentals=0),
        name=name,
    )(*operands)


def body(volume, kernel_one, bias_one, kernel_two, bias_two):
    b1, b2 = bias_one.reshape(1, -1), bias_two.reshape(1, -1)
    rows, odd = volume.shape[0], lax.axis_index("depth") % 2
    sides = 1 if lax.axis_size("filt") == 2 else 2

    tall, k0 = gathered(volume, "filt", "height", kernel_one[:1])
    own, wide = volume.shape[2] // lax.axis_size("filt"), bias_one.shape[0]
    shape = (rows, volume.shape[1] + 4, own, wide)
    near, far = exchange(depth_rows(tall, 0, rows, own), depth_rows(tall, rows - 2, rows, own), "depth")
    out_near, keep, k1, k2 = kernel_call(near_kernel, "near", rows + 2, sides, shape, True, (tall, near, k0, kernel_one, b1, kernel_two, b2))
    shard = volume.shape[3]
    def pieces(y):
        f, n = lax.axis_index("filt"), lax.axis_size("filt")
        return [lax.dynamic_slice_in_dim(y, (f + s) % n * shard, shard, 3) for s in range(n)]
    out_far, = kernel_call(far_kernel, "far", 4, sides, shape, False, (tall, far, keep, k1, b1, k2, b2))
    out = jnp.where(odd == 1, jnp.concatenate([out_near, out_far], 0), jnp.concatenate([out_far, out_near], 0))
    return by_origin(swapped(pieces(out), "filt"), "filt", 2)


def solution(mesh):
    in_specs = (P("depth", "height", None, "filt"), P(), P(), P(), P())
    out_specs = P("depth", "height", None, "filt")
    return jax.shard_map(body, mesh=mesh, in_specs=in_specs, out_specs=out_specs, check_vma=False)
```

```python
import functools

import jax
import jax.numpy as jnp
from jax import lax
from jax.experimental import pallas as pl
from jax.experimental.pallas import tpu as pltpu
from jax.sharding import PartitionSpec as P

VMEM = pl.BlockSpec(memory_space=pltpu.VMEM)
HBM = pl.BlockSpec(memory_space=pltpu.HBM)


def leaky(value):
    return jnp.where(value > 0, value, 0.3 * value)


def pairings(peers):
    rounds = []
    for start in (0, 1):
        pairs = [(i, i + 1) for i in range(start, peers - 1, 2)]
        busy = {i for pair in pairs for i in pair}
        rounds.append(pairs + [(j, i) for i, j in pairs] + [(i, i) for i in range(peers) if i not in busy])
    return rounds


def exchange(first, last, axis):
    odd = lax.axis_index(axis) % 2 == 1
    near, far = pairings(lax.axis_size(axis))
    one = lax.ppermute(jnp.where(odd, first, last), axis, near)
    two = lax.ppermute(jnp.where(odd, last, first), axis, far)
    return one, two


def beside(one, two, axis):
    peers, index = lax.axis_size(axis), lax.axis_index(axis)
    odd = index % 2 == 1
    before = jnp.where(odd, one, two)
    after = jnp.where(odd, two, one)
    before = jnp.where(index == 0, jnp.zeros_like(before), before)
    after = jnp.where(index == peers - 1, jnp.zeros_like(after), after)
    return before, after


def by_origin(parts, axis, dim):
    peers, index = lax.axis_size(axis), lax.axis_index(axis)
    if peers == 2:
        return jnp.where(index == 0, jnp.concatenate(parts, dim), jnp.concatenate(parts[::-1], dim))
    stacked = jnp.stack(parts)
    order = (index - jnp.arange(peers)) % peers
    return jnp.concatenate([stacked[order[c]] for c in range(peers)], dim)


def swapped(pieces, axis):
    peers = lax.axis_size(axis)
    moves = [[(i, (i + s) % peers) for i in range(peers)] for s in range(peers)]
    return [pieces[0]] + [lax.ppermute(pieces[s], axis, moves[s]) for s in range(1, peers)]


def in_order(parts, axis):
    return by_origin(parts, axis, 3)


def gathered(x, columns, rows, extra):
    nc, nr = lax.axis_size(columns), lax.axis_size(rows)
    c, r = lax.axis_index(columns), lax.axis_index(rows)
    own, shard = x.shape[2] // nc, x.shape[3]
    odd = r % 2 == 1

    def window(s, x):
        block = (c + s) % nc
        if nc == 2:
            return jnp.where(block == 0, x[:, :, :own + 8], x[:, :, own - 8:])
        padded = jnp.pad(x, ((0, 0), (0, 0), (2, 2), (0, 0)))
        return lax.dynamic_slice_in_dim(padded, block * own, own + 4, 2)

    def halves(s, near):
        block = (c + s) % nc
        if nc == 2:
            main = jnp.where(block == 0, near[:, :, :own], near[:, :, 8:])
            ends = jnp.where(block == 0, near[:, :, own:own + 2], near[:, :, 6:8])
        else:
            main, ends = near[:, :, 2:-2], jnp.concatenate([near[:, :, :2], near[:, :, -2:]], 2)

        def flat(rows):
            return jnp.concatenate([main[:, rows].reshape(-1, shard), ends[:, rows].reshape(-1, shard)], 0)
        first, last = flat(slice(0, 2)), flat(slice(2, 4))
        return jnp.where(odd, first, last), jnp.where(odd, last, first)

    windows = lax.optimization_barrier([window(s, x) for s in range(1, nc)])
    sent = [halves(s, windows[s - 1]) for s in range(1, nc)]
    again, extra = lax.optimization_barrier((x, extra))
    kept = halves(0, lax.optimization_barrier(window(0, again)))
    got = []
    for r_ in range(2):
        parts = [kept[r_]] + [lax.ppermute(sent[s - 1][r_], columns, [(i, (i + s) % nc) for i in range(nc)]) for s in range(1, nc)]
        got.append(by_origin(parts, columns, 1))
    near, far = pairings(nr)
    one = lax.ppermute(got[0], rows, near)
    two = lax.ppermute(got[1], rows, far)
    before, after = beside(one, two, rows)
    inner = jnp.where(odd, jnp.stack(got), jnp.stack(got[::-1]))
    return jnp.concatenate([before[None], inner, after[None]], 0), extra


def depth_rows(pairs, first, depth, own):
    ends = pairs.shape[1] // depth // 2 - own
    at = 2 * first * own, 2 * (depth * own + first * ends)
    main = pairs[:, at[0]:at[0] + 4 * own].reshape(-1, pairs.shape[2])
    return jnp.concatenate([main, pairs[:, at[1]:at[1] + 4 * ends].reshape(-1, pairs.shape[2])], 0)


def from_pairs(ref, own, depth):
    def row(d):
        pairs, C = ref.shape[0], ref.shape[2]
        ends = ref.shape[1] // depth // 2 - own
        main = [ref[p, 2 * d * own:2 * (d + 1) * own, :].reshape(2, own, C) for p in range(pairs)]
        tail = [ref[p, 2 * depth * own:, :].astype(jnp.float32)[2 * d * ends:2 * (d + 1) * ends] for p in range(pairs)]
        return jnp.concatenate(main, 0), tail
    return row


def from_rows(ref, own, pairs):
    def row(d):
        C = ref.shape[1]
        ends = ref.shape[0] // pairs // 4 - own
        main = [ref[(2 * p + d) * 2 * own:(2 * p + d + 1) * 2 * own, :].reshape(2, own, C) for p in range(pairs)]
        tail = ref[4 * pairs * own:, :].astype(jnp.float32)
        return jnp.concatenate(main, 0), [tail[(2 * p + d) * 2 * ends:(2 * p + d + 1) * 2 * ends] for p in range(pairs)]
    return row


def either(odd, one, two):
    return jax.tree.map(lambda a, b: jnp.where(odd == 1, a, b), one, two)


def spread(source, rows, at, sides, info, x3, ef, et, eb):
    H, own, C = x3.shape[1], x3.shape[2], x3.shape[3] // 3
    column = lax.broadcasted_iota(jnp.int32, (own, C), 0)
    f, none = info[4], jnp.zeros((H, C), jnp.float32)
    ends = 2 * sides
    for d in range(rows):
        x, tail = source(d)
        row = at + d
        picks = [x[:, own - 1:own, :], x[:, 0:1, :]]
        if sides == 1:
            picks = [jnp.where(f == 0, picks[0], picks[1])]
        edge = [[] for _ in range(ends + len(picks))]
        for l in range(0, C, 128):
            for p, part in enumerate(tail):
                et[l // 128, 2 * p * ends:2 * (p + 1) * ends, :] = part[:, l:l + 128]
            for e in range(ends):
                edge[e].append(et[l // 128, pl.ds(e, H, stride=ends), :])
            for k, pick in enumerate(picks):
                for h in range(H):
                    ef[k, l // 128, h * 8:h * 8 + 1, :] = pick[h, :, l:l + 128].astype(jnp.float32)
                edge[ends + k].append(ef[k, l // 128, pl.ds(0, H, stride=8), :])
        edge = [jnp.concatenate(e, 1) for e in edge]
        if sides == 1:
            e0, e1, inner = edge
            left, right = jnp.where(f == 0, none, e1), jnp.where(f == 0, e0, none)
            taps = [[jnp.where(f == 0, inner, e0), jnp.where(f == 0, e0, e1), jnp.where(f == 0, e1, inner)]]
        else:
            l0, l1, r0, r1, last, first = edge
            left, right = l1, r0
            taps = [[l0, l1, first], [last, r0, r1]]
        for s in range(sides):
            wide = jnp.concatenate(taps[s], 1)
            for b in range(3):
                moved = wide if b == 0 else pltpu.roll(wide, H - b, 0)
                eb[s, b, row] = moved.astype(jnp.bfloat16)
        for h in range(H):
            line = x[h].astype(jnp.float32)
            x3[row, h, :, 0:C] = jnp.where(column == 0, left[h:h + 1], pltpu.roll(line, 1, 0)).astype(jnp.bfloat16)
            x3[row, h, :, C:2 * C] = x[h]
            x3[row, h, :, 2 * C:] = jnp.where(column == own - 1, right[h:h + 1], pltpu.roll(line, own - 1, 0)).astype(jnp.bfloat16)


def clear(rows, at, x3, eb):
    for d in range(rows):
        x3[at + d] = jnp.zeros(x3.shape[1:], x3.dtype)
        for s in range(eb.shape[0]):
            for b in range(3):
                eb[s, b, at + d] = jnp.zeros(eb.shape[3:], eb.dtype)


def hidden_sums(d, taps, ends, x3, eb, k1, acc):
    H, own, C = x3.shape[1], x3.shape[2], x3.shape[3] // 3
    main = (H - 2) * own
    for a in taps:
        for b in range(3):
            lhs = [x3[d + a, b:b + H - 2].reshape(main, 3 * C)]
            if ends:
                lhs += [eb[s, b, a:a + ends].reshape(ends * H, 3 * C) for s in range(eb.shape[0])]
            acc += jnp.dot(jnp.concatenate(lhs, 0), k1[a, b].reshape(3 * C, C), preferred_element_type=jnp.float32)
    return acc


def hidden_rows(d, at, depth, sides, info, own, H, raw, ends, h3):
    C = raw.shape[2]
    count = ends.shape[0] // (sides * H)
    column = lax.broadcasted_iota(jnp.int32, (own, C), 0)
    none = jnp.zeros((1, C), jnp.float32)
    inside = jnp.logical_and(depth >= 0, depth < info[1])
    for h in range(H - 2):
        ok = inside
        if h == 0:
            ok = jnp.logical_and(ok, info[2] == 0)
        if h == H - 3:
            ok = jnp.logical_and(ok, info[3] == 0)
        row = jnp.where(ok, raw[d, h * own:(h + 1) * own, :], 0.0)
        edge = [ends[(s * count + d) * H + h:(s * count + d) * H + h + 1, :] for s in range(sides)]
        left = jnp.where(jnp.logical_and(ok, info[4] > 0), edge[0], none)
        right = jnp.where(jnp.logical_and(ok, info[4] < info[5] - 1), edge[sides - 1], none)
        h3[at, h, :, 0:C] = jnp.where(column == 0, left, pltpu.roll(row, 1, 0)).astype(jnp.bfloat16)
        h3[at, h, :, C:2 * C] = row.astype(jnp.bfloat16)
        h3[at, h, :, 2 * C:] = jnp.where(column == own - 1, right, pltpu.roll(row, own - 1, 0)).astype(jnp.bfloat16)


def hidden_part(d, taps, x3, eb, k1, bias, raw, ends):
    main, C = raw.shape[1:]
    size = ends.shape[0] if d == 0 else 0
    if taps[0] == 0:
        acc = jnp.zeros((main + size, C), jnp.float32)
    else:
        acc = jnp.concatenate([raw[d], ends[...]], 0) if size else raw[d]
    acc = hidden_sums(d, taps, raw.shape[0] if size else 0, x3, eb, k1, acc)
    if taps[-1] == 2:
        acc = leaky(acc + bias[...])
    raw[d] = acc[:main]
    if size:
        ends[...] = acc[main:]


def feature_sums(terms, k2, acc):
    for pair, a in terms:
        H1, own, C = pair.shape[1], pair.shape[2], pair.shape[3] // 3
        H0 = H1 - 2
        for b in range(3):
            lhs = pair[:, b:b + H0].reshape(2 * H0 * own, 3 * C)
            acc += jnp.dot(lhs, k2[a, b].reshape(3 * C, C), preferred_element_type=jnp.float32)
    return acc


def features(acc, bias, o_ref):
    o_ref[...] = leaky(acc + bias[...]).astype(jnp.bfloat16).reshape(o_ref.shape)


def places(rows):
    d, h, f = (lax.axis_index(a) for a in ("depth", "height", "filt"))
    nd, nh, nf = (lax.axis_size(a) for a in ("depth", "height", "filt"))
    odd = lax.rem(d, 2)
    end = (d == nd - 1).astype(jnp.int32)
    start = (d == 0).astype(jnp.int32)
    return (d * rows, nd * rows, (h == 0).astype(jnp.int32), (h == nh - 1).astype(jnp.int32), f, nf, odd,
            end * (1 - odd), jnp.where(odd == 1, end, start))


def near_kernel(sides, depth, xc, xn, k0, k1h, b1, k2h, b2, o_ref, keep, k1, k2, x3, ef, et, eb, h3, raw, ends, total, sems):
    copies = [pltpu.make_async_copy(k1h.at[a], k1.at[a], sems.at[a]) for a in range(3)]
    copies += [pltpu.make_async_copy(k2h.at[a], k2.at[a], sems.at[3 + a]) for a in range(3)]
    for copy in copies[1:3]:
        copy.start()
    D, H, own = depth, x3.shape[1], x3.shape[2]
    info = places(D)
    odd = info[6]
    scratch = (x3, ef, et, eb)
    spread(from_pairs(xc, own, D), D, 2 * odd, sides, info, *scratch)
    spread(from_rows(xn, own, H // 2), 2, D * (1 - odd), sides, info, *scratch)

    @pl.when(info[7] > 0)
    def _():
        clear(2, D * (1 - odd), x3, eb)

    first = info[0] - 1 + 2 * (1 - odd)

    def block(run):
        pl.when(odd >= 0)(run)

    def part(d, taps):
        hidden_part(d, taps, x3, eb, k1 if taps[0] else k0, b1, raw, ends)

    def rows(d):
        hidden_rows(d, d, first + d, sides, info, own, H, raw, ends, h3)

    for a in range(3):
        if a > 0:
            copies[a].wait()
        if a == 1:
            for copy in copies[3:] + copies[:1]:
                copy.start()

        @block
        def _():
            for d in range(D):
                part(d, [a])
                if a == 2:
                    rows(d)
    for copy in copies[3:] + copies[:1]:
        copy.wait()

    @block
    def _():
        keep[...] = h3[pl.ds((D - 2) * odd, 2)]
        features(feature_sums([(h3.at[a:a + 2], a) for a in range(3)], k2, jnp.zeros(total.shape, jnp.float32)), b2, o_ref)


def far_kernel(sides, depth, xc, xf, keep, k1, b1, k2, b2, o_ref, x3, ef, et, eb, h3, raw, ends, total):
    D, H, own = depth, x3.shape[1], x3.shape[2]
    info = places(D)
    odd = info[6]
    scratch = (x3, ef, et, eb)
    tall = from_pairs(xc, own, D)
    first = info[0] - 1 + D * odd
    known = 2 * (1 - odd)

    @pl.when(odd >= 0)
    def _():
        spread(lambda d: either(odd, tall(D - 2 + d), tall(d)), 2, 2 * (1 - odd), sides, info, *scratch)
        spread(from_rows(xf, own, H // 2), 2, 2 * odd, sides, info, *scratch)
        total[...] = feature_sums([(keep, known)], k2, jnp.zeros(total.shape, jnp.float32))
        h3[pl.ds(known, 2)] = keep[...]

    @pl.when(info[8] > 0)
    def _():
        clear(2, 2 * odd, x3, eb)

    @pl.when(odd >= 0)
    def _():
        for d in range(2):
            hidden_part(d, range(3), x3, eb, k1, b1, raw, ends)
        for d in range(2):
            hidden_rows(d, 2 * odd + d, first + d, sides, info, own, H, raw, ends, h3)

    @pl.when(odd >= 0)
    def _():
        features(feature_sums([(h3.at[1:3], 1), (h3.at[pl.ds(2 * odd, 2)], 2 * odd)], k2, total[...]), b2, o_ref)


def kernel_call(kernel, name, rows, sides, shape, near, operands):
    D, H, own, C = shape
    weights = jax.ShapeDtypeStruct((3, 3, 3, C, C), jnp.bfloat16)
    out = [jax.ShapeDtypeStruct((2, H - 4, own, C), jnp.bfloat16)]
    scratch = [
        pltpu.VMEM((rows, H, own, 3 * C), jnp.bfloat16),
        pltpu.VMEM((sides, C // 128, H * 8, 128), jnp.float32),
        pltpu.VMEM((C // 128, 2 * sides * H, 128), jnp.float32),
        pltpu.VMEM((sides, 3, rows, H, 3 * C), jnp.bfloat16),
        pltpu.VMEM((4, H - 2, own, 3 * C), jnp.bfloat16),
        pltpu.VMEM((rows - 2, (H - 2) * own, C), jnp.float32),
        pltpu.VMEM((sides * (rows - 2) * H, C), jnp.float32),
        pltpu.VMEM((2 * (H - 4) * own, C), jnp.float32),
    ]
    specs = [VMEM] * len(operands)
    if near:
        out += [jax.ShapeDtypeStruct((2, H - 2, own, 3 * C), jnp.bfloat16), weights, weights]
        scratch.append(pltpu.SemaphoreType.DMA((6,)))
        specs[3] = specs[5] = HBM
    hid = (rows - 2) * (H - 2) * own
    return pl.pallas_call(
        functools.partial(kernel, sides, D),
        out_shape=out,
        in_specs=specs,
        out_specs=[VMEM] * len(out),
        scratch_shapes=scratch,
        compiler_params=pltpu.CompilerParams(vmem_limit_bytes=(43 if near else 24) * 2**20),
        cost_estimate=pl.CostEstimate(flops=2 * 27 * C * C * (hid + 2 * (H - 4) * own), bytes_accessed=2**20, transcendentals=0),
        name=name,
    )(*operands)


def body(volume, kernel_one, bias_one, kernel_two, bias_two):
    b1, b2 = bias_one.reshape(1, -1), bias_two.reshape(1, -1)
    rows, odd = volume.shape[0], lax.axis_index("depth") % 2
    sides = 1 if lax.axis_size("filt") == 2 else 2

    tall, k0 = gathered(volume, "filt", "height", kernel_one[:1])
    own, wide = volume.shape[2] // lax.axis_size("filt"), bias_one.shape[0]
    shape = (rows, volume.shape[1] + 4, own, wide)
    near, far = exchange(depth_rows(tall, 0, rows, own), depth_rows(tall, rows - 2, rows, own), "depth")
    out_near, keep, k1, k2 = kernel_call(near_kernel, "near", rows + 2, sides, shape, True, (tall, near, k0, kernel_one, b1, kernel_two, b2))
    shard = volume.shape[3]
    def pieces(y):
        f, n = lax.axis_index("filt"), lax.axis_size("filt")
        return [lax.dynamic_slice_in_dim(y, (f + s) % n * shard, shard, 3) for s in range(n)]
    out_far, = kernel_call(far_kernel, "far", 4, sides, shape, False, (tall, far, keep, k1, b1, k2, b2))
    out = jnp.where(odd == 1, jnp.concatenate([out_near, out_far], 0), jnp.concatenate([out_far, out_near], 0))
    return by_origin(swapped(pieces(out), "filt"), "filt", 2)


def solution(mesh):
    in_specs = (P("depth", "height", None, "filt"), P(), P(), P(), P())
    out_specs = P("depth", "height", None, "filt")
    return jax.shard_map(body, mesh=mesh, in_specs=in_specs, out_specs=out_specs, check_vma=False)
```

```python
import functools

import jax
import jax.numpy as jnp
from jax import lax
from jax.experimental import pallas as pl
from jax.experimental.pallas import tpu as pltpu
from jax.sharding import PartitionSpec as P

VMEM = pl.BlockSpec(memory_space=pltpu.VMEM)
HBM = pl.BlockSpec(memory_space=pltpu.HBM)


def leaky(value):
    return jnp.where(value > 0, value, 0.3 * value)


def pairings(peers):
    rounds = []
    for start in (0, 1):
        pairs = [(i, i + 1) for i in range(start, peers - 1, 2)]
        busy = {i for pair in pairs for i in pair}
        rounds.append(pairs + [(j, i) for i, j in pairs] + [(i, i) for i in range(peers) if i not in busy])
    return rounds


def exchange(first, last, axis):
    odd = lax.axis_index(axis) % 2 == 1
    near, far = pairings(lax.axis_size(axis))
    one = lax.ppermute(jnp.where(odd, first, last), axis, near)
    two = lax.ppermute(jnp.where(odd, last, first), axis, far)
    return one, two


def beside(one, two, axis):
    peers, index = lax.axis_size(axis), lax.axis_index(axis)
    odd = index % 2 == 1
    before = jnp.where(odd, one, two)
    after = jnp.where(odd, two, one)
    before = jnp.where(index == 0, jnp.zeros_like(before), before)
    after = jnp.where(index == peers - 1, jnp.zeros_like(after), after)
    return before, after


def by_origin(parts, axis, dim):
    peers, index = lax.axis_size(axis), lax.axis_index(axis)
    if peers == 2:
        return jnp.where(index == 0, jnp.concatenate(parts, dim), jnp.concatenate(parts[::-1], dim))
    stacked = jnp.stack(parts)
    order = (index - jnp.arange(peers)) % peers
    return jnp.concatenate([stacked[order[c]] for c in range(peers)], dim)


def swapped(pieces, axis):
    peers = lax.axis_size(axis)
    moves = [[(i, (i + s) % peers) for i in range(peers)] for s in range(peers)]
    return [pieces[0]] + [lax.ppermute(pieces[s], axis, moves[s]) for s in range(1, peers)]


def in_order(parts, axis):
    return by_origin(parts, axis, 3)


def gathered(x, columns, rows, extra):
    nc, nr = lax.axis_size(columns), lax.axis_size(rows)
    c, r = lax.axis_index(columns), lax.axis_index(rows)
    own, shard = x.shape[2] // nc, x.shape[3]
    odd = r % 2 == 1

    def window(s, x):
        block = (c + s) % nc
        if nc == 2:
            return jnp.where(block == 0, x[:, :, :own + 8], x[:, :, own - 8:])
        padded = jnp.pad(x, ((0, 0), (0, 0), (2, 2), (0, 0)))
        return lax.dynamic_slice_in_dim(padded, block * own, own + 4, 2)

    def halves(s, near):
        block = (c + s) % nc
        if nc == 2:
            main = jnp.where(block == 0, near[:, :, :own], near[:, :, 8:])
            ends = jnp.where(block == 0, near[:, :, own:own + 2], near[:, :, 6:8])
        else:
            main, ends = near[:, :, 2:-2], jnp.concatenate([near[:, :, :2], near[:, :, -2:]], 2)

        def flat(rows):
            return jnp.concatenate([main[:, rows].reshape(-1, shard), ends[:, rows].reshape(-1, shard)], 0)
        first, last = flat(slice(0, 2)), flat(slice(2, 4))
        return jnp.where(odd, first, last), jnp.where(odd, last, first)

    windows = lax.optimization_barrier([window(s, x) for s in range(1, nc)])
    sent = [halves(s, windows[s - 1]) for s in range(1, nc)]
    again, extra = lax.optimization_barrier((x, extra))
    kept = halves(0, lax.optimization_barrier(window(0, again)))
    got = []
    for r_ in range(2):
        parts = [kept[r_]] + [lax.ppermute(sent[s - 1][r_], columns, [(i, (i + s) % nc) for i in range(nc)]) for s in range(1, nc)]
        got.append(by_origin(parts, columns, 1))
    near, far = pairings(nr)
    one = lax.ppermute(got[0], rows, near)
    two = lax.ppermute(got[1], rows, far)
    before, after = beside(one, two, rows)
    inner = jnp.where(odd, jnp.stack(got), jnp.stack(got[::-1]))
    return jnp.concatenate([before[None], inner, after[None]], 0), extra


def depth_rows(pairs, first, depth, own):
    ends = pairs.shape[1] // depth // 2 - own
    at = 2 * first * own, 2 * (depth * own + first * ends)
    main = pairs[:, at[0]:at[0] + 4 * own].reshape(-1, pairs.shape[2])
    return jnp.concatenate([main, pairs[:, at[1]:at[1] + 4 * ends].reshape(-1, pairs.shape[2])], 0)


def from_pairs(ref, own, depth):
    def row(d):
        pairs, C = ref.shape[0], ref.shape[2]
        ends = ref.shape[1] // depth // 2 - own
        main = [ref[p, 2 * d * own:2 * (d + 1) * own, :].reshape(2, own, C) for p in range(pairs)]
        tail = [ref[p, 2 * depth * own:, :].astype(jnp.float32)[2 * d * ends:2 * (d + 1) * ends] for p in range(pairs)]
        return jnp.concatenate(main, 0), tail
    return row


def from_rows(ref, own, pairs):
    def row(d):
        C = ref.shape[1]
        ends = ref.shape[0] // pairs // 4 - own
        main = [ref[(2 * p + d) * 2 * own:(2 * p + d + 1) * 2 * own, :].reshape(2, own, C) for p in range(pairs)]
        tail = ref[4 * pairs * own:, :].astype(jnp.float32)
        return jnp.concatenate(main, 0), [tail[(2 * p + d) * 2 * ends:(2 * p + d + 1) * 2 * ends] for p in range(pairs)]
    return row


def either(odd, one, two):
    return jax.tree.map(lambda a, b: jnp.where(odd == 1, a, b), one, two)


def spread(source, rows, at, sides, info, x3, ef, et, eb):
    H, own, C = x3.shape[1], x3.shape[2], x3.shape[3] // 3
    column = lax.broadcasted_iota(jnp.int32, (own, C), 0)
    f, none = info[4], jnp.zeros((H, C), jnp.float32)
    ends = 2 * sides
    for d in range(rows):
        x, tail = source(d)
        row = at + d
        picks = [x[:, own - 1:own, :], x[:, 0:1, :]]
        if sides == 1:
            picks = [jnp.where(f == 0, picks[0], picks[1])]
        edge = [[] for _ in range(ends + len(picks))]
        for l in range(0, C, 128):
            for p, part in enumerate(tail):
                et[l // 128, 2 * p * ends:2 * (p + 1) * ends, :] = part[:, l:l + 128]
            for e in range(ends):
                edge[e].append(et[l // 128, pl.ds(e, H, stride=ends), :])
            for k, pick in enumerate(picks):
                for h in range(H):
                    ef[k, l // 128, h * 8:h * 8 + 1, :] = pick[h, :, l:l + 128].astype(jnp.float32)
                edge[ends + k].append(ef[k, l // 128, pl.ds(0, H, stride=8), :])
        edge = [jnp.concatenate(e, 1) for e in edge]
        if sides == 1:
            e0, e1, inner = edge
            left, right = jnp.where(f == 0, none, e1), jnp.where(f == 0, e0, none)
            taps = [[jnp.where(f == 0, inner, e0), jnp.where(f == 0, e0, e1), jnp.where(f == 0, e1, inner)]]
        else:
            l0, l1, r0, r1, last, first = edge
            left, right = l1, r0
            taps = [[l0, l1, first], [last, r0, r1]]
        for s in range(sides):
            wide = jnp.concatenate(taps[s], 1)
            for b in range(3):
                moved = wide if b == 0 else pltpu.roll(wide, H - b, 0)
                eb[s, b, row] = moved.astype(jnp.bfloat16)
        for h in range(H):
            line = x[h].astype(jnp.float32)
            x3[row, h, :, 0:C] = jnp.where(column == 0, left[h:h + 1], pltpu.roll(line, 1, 0)).astype(jnp.bfloat16)
            x3[row, h, :, C:2 * C] = x[h]
            x3[row, h, :, 2 * C:] = jnp.where(column == own - 1, right[h:h + 1], pltpu.roll(line, own - 1, 0)).astype(jnp.bfloat16)


def clear(rows, at, x3, eb):
    for d in range(rows):
        x3[at + d] = jnp.zeros(x3.shape[1:], x3.dtype)
        for s in range(eb.shape[0]):
            for b in range(3):
                eb[s, b, at + d] = jnp.zeros(eb.shape[3:], eb.dtype)


def hidden_sums(d, taps, ends, x3, eb, k1, acc):
    H, own, C = x3.shape[1], x3.shape[2], x3.shape[3] // 3
    main = (H - 2) * own
    for a in taps:
        for b in range(3):
            lhs = [x3[d + a, b:b + H - 2].reshape(main, 3 * C)]
            if ends:
                lhs += [eb[s, b, a:a + ends].reshape(ends * H, 3 * C) for s in range(eb.shape[0])]
            acc += jnp.dot(jnp.concatenate(lhs, 0), k1[a, b].reshape(3 * C, C), preferred_element_type=jnp.float32)
    return acc


def hidden_rows(d, at, depth, sides, info, own, H, raw, ends, h3):
    C = raw.shape[2]
    count = ends.shape[0] // (sides * H)
    column = lax.broadcasted_iota(jnp.int32, (own, C), 0)
    none = jnp.zeros((1, C), jnp.float32)
    inside = jnp.logical_and(depth >= 0, depth < info[1])
    for h in range(H - 2):
        ok = inside
        if h == 0:
            ok = jnp.logical_and(ok, info[2] == 0)
        if h == H - 3:
            ok = jnp.logical_and(ok, info[3] == 0)
        row = jnp.where(ok, raw[d, h * own:(h + 1) * own, :], 0.0)
        edge = [ends[(s * count + d) * H + h:(s * count + d) * H + h + 1, :] for s in range(sides)]
        left = jnp.where(jnp.logical_and(ok, info[4] > 0), edge[0], none)
        right = jnp.where(jnp.logical_and(ok, info[4] < info[5] - 1), edge[sides - 1], none)
        h3[at, h, :, 0:C] = jnp.where(column == 0, left, pltpu.roll(row, 1, 0)).astype(jnp.bfloat16)
        h3[at, h, :, C:2 * C] = row.astype(jnp.bfloat16)
        h3[at, h, :, 2 * C:] = jnp.where(column == own - 1, right, pltpu.roll(row, own - 1, 0)).astype(jnp.bfloat16)


def hidden_part(d, taps, x3, eb, k1, bias, raw, ends, outer):
    main, C = raw.shape[1:]
    size = ends.shape[0] if outer else 0
    if taps[0] == 0:
        acc = jnp.zeros((main + size, C), jnp.float32)
    else:
        acc = jnp.concatenate([raw[d], ends[...]], 0) if size else raw[d]
    acc = hidden_sums(d, taps, raw.shape[0] if size else 0, x3, eb, k1, acc)
    if taps[-1] == 2:
        acc = leaky(acc + bias[...])
    raw[d] = acc[:main]
    if size:
        ends[...] = acc[main:]


def feature_sums(terms, k2, acc):
    for pair, a in terms:
        H1, own, C = pair.shape[1], pair.shape[2], pair.shape[3] // 3
        H0 = H1 - 2
        for b in range(3):
            lhs = pair[:, b:b + H0].reshape(2 * H0 * own, 3 * C)
            acc += jnp.dot(lhs, k2[a, b].reshape(3 * C, C), preferred_element_type=jnp.float32)
    return acc


def features(acc, bias, o_ref):
    o_ref[...] = leaky(acc + bias[...]).astype(jnp.bfloat16).reshape(o_ref.shape)


def places(rows):
    d, h, f = (lax.axis_index(a) for a in ("depth", "height", "filt"))
    nd, nh, nf = (lax.axis_size(a) for a in ("depth", "height", "filt"))
    odd = lax.rem(d, 2)
    end = (d == nd - 1).astype(jnp.int32)
    start = (d == 0).astype(jnp.int32)
    return (d * rows, nd * rows, (h == 0).astype(jnp.int32), (h == nh - 1).astype(jnp.int32), f, nf, odd,
            end * (1 - odd), jnp.where(odd == 1, end, start))


def near_kernel(sides, depth, xc, xn, k0, k1h, b1, k2h, b2, o_ref, keep, part_sum, k1, k2, x3, ef, et, eb, h3, raw, ends, total, sems):
    copies = [pltpu.make_async_copy(k1h.at[a], k1.at[a], sems.at[a]) for a in range(3)]
    copies += [pltpu.make_async_copy(k2h.at[a], k2.at[a], sems.at[3 + a]) for a in range(3)]
    for copy in copies[1:3]:
        copy.start()
    D, H, own = depth, x3.shape[1], x3.shape[2]
    info = places(D)
    odd = info[6]
    scratch = (x3, ef, et, eb)
    tall, near = from_pairs(xc, own, D), from_rows(xn, own, H // 2)

    def lay(r):
        def source(_):
            if r < 2:
                return either(odd, near(r), tall(r))
            return either(odd, tall(r - 2), tall(r) if r < D else near(r - D))
        spread(source, 1, r, sides, info, *scratch)

    first = info[0] - 1 + 2 * (1 - odd)

    def block(run):
        pl.when(odd >= 0)(run)

    def part(d, taps):
        hidden_part(d, taps, x3, eb, k1 if taps[0] else k0, b1, raw, ends, d == (0 if taps[0] else D - 1))

    def rows(d):
        hidden_rows(d, d, first + d, sides, info, own, H, raw, ends, h3)

    for a in range(3):
        if a > 0:
            copies[a].wait()
        if a == 1:
            for copy in copies[3:] + copies[:1]:
                copy.start()

        @block
        def _():
            for d in range(D):
                if a == 0:
                    lay(d)
                part(d, [a])
                if a == 2:
                    rows(d)
            if a == 0:
                lay(D)
                lay(D + 1)

        if a == 0:
            @pl.when(info[7] > 0)
            def _():
                clear(2, D, x3, eb)
    for copy in copies[3:] + copies[:1]:
        copy.wait()

    @block
    def _():
        keep[...] = h3[pl.ds((D - 2) * odd, 2)]
        part_sum[...] = feature_sums([(h3.at[pl.ds((D - 2) * odd, 2)], 2 * (1 - odd))], k2, jnp.zeros(part_sum.shape, jnp.float32))
        features(feature_sums([(h3.at[a:a + 2], a) for a in range(3)], k2, jnp.zeros(total.shape, jnp.float32)), b2, o_ref)


def far_kernel(sides, depth, xc, xf, keep, part_sum, k1, b1, k2, b2, o_ref, x3, ef, et, eb, h3, raw, ends, total):
    D, H, own = depth, x3.shape[1], x3.shape[2]
    info = places(D)
    odd = info[6]
    scratch = (x3, ef, et, eb)
    tall = from_pairs(xc, own, D)
    first = info[0] - 1 + D * odd
    known = 2 * (1 - odd)

    @pl.when(odd >= 0)
    def _():
        spread(lambda d: either(odd, tall(D - 2 + d), tall(d)), 2, 2 * (1 - odd), sides, info, *scratch)
        spread(from_rows(xf, own, H // 2), 2, 2 * odd, sides, info, *scratch)
        h3[pl.ds(known, 2)] = keep[...]

    @pl.when(info[8] > 0)
    def _():
        clear(2, 2 * odd, x3, eb)

    @pl.when(odd >= 0)
    def _():
        for d in range(2):
            hidden_part(d, range(3), x3, eb, k1, b1, raw, ends, d == 0)
        for d in range(2):
            hidden_rows(d, 2 * odd + d, first + d, sides, info, own, H, raw, ends, h3)

    @pl.when(odd >= 0)
    def _():
        features(feature_sums([(h3.at[1:3], 1), (h3.at[pl.ds(2 * odd, 2)], 2 * odd)], k2, part_sum[...]), b2, o_ref)


def kernel_call(kernel, name, rows, sides, shape, near, operands):
    D, H, own, C = shape
    weights = jax.ShapeDtypeStruct((3, 3, 3, C, C), jnp.bfloat16)
    out = [jax.ShapeDtypeStruct((2, H - 4, own, C), jnp.bfloat16)]
    scratch = [
        pltpu.VMEM((rows, H, own, 3 * C), jnp.bfloat16),
        pltpu.VMEM((sides, C // 128, H * 8, 128), jnp.float32),
        pltpu.VMEM((C // 128, 2 * sides * H, 128), jnp.float32),
        pltpu.VMEM((sides, 3, rows, H, 3 * C), jnp.bfloat16),
        pltpu.VMEM((4, H - 2, own, 3 * C), jnp.bfloat16),
        pltpu.VMEM((rows - 2, (H - 2) * own, C), jnp.float32),
        pltpu.VMEM((sides * (rows - 2) * H, C), jnp.float32),
        pltpu.VMEM((2 * (H - 4) * own, C), jnp.float32),
    ]
    specs = [VMEM] * len(operands)
    if near:
        out += [jax.ShapeDtypeStruct((2, H - 2, own, 3 * C), jnp.bfloat16), jax.ShapeDtypeStruct((2 * (H - 4) * own, C), jnp.float32), weights, weights]
        scratch.append(pltpu.SemaphoreType.DMA((6,)))
        specs[3] = specs[5] = HBM
    hid = (rows - 2) * (H - 2) * own
    return pl.pallas_call(
        functools.partial(kernel, sides, D),
        out_shape=out,
        in_specs=specs,
        out_specs=[VMEM] * len(out),
        scratch_shapes=scratch,
        compiler_params=pltpu.CompilerParams(vmem_limit_bytes=(43 if near else 24) * 2**20),
        cost_estimate=pl.CostEstimate(flops=2 * 27 * C * C * (hid + 2 * (H - 4) * own), bytes_accessed=2**20, transcendentals=0),
        name=name,
    )(*operands)


def body(volume, kernel_one, bias_one, kernel_two, bias_two):
    b1, b2 = bias_one.reshape(1, -1), bias_two.reshape(1, -1)
    rows, odd = volume.shape[0], lax.axis_index("depth") % 2
    sides = 1 if lax.axis_size("filt") == 2 else 2

    tall, k0 = gathered(volume, "filt", "height", kernel_one[:1])
    own, wide = volume.shape[2] // lax.axis_size("filt"), bias_one.shape[0]
    shape = (rows, volume.shape[1] + 4, own, wide)
    near, far = exchange(depth_rows(tall, 0, rows, own), depth_rows(tall, rows - 2, rows, own), "depth")
    out_near, keep, part_sum, k1, k2 = kernel_call(near_kernel, "near", rows + 2, sides, shape, True, (tall, near, k0, kernel_one, b1, kernel_two, b2))
    shard = volume.shape[3]
    def pieces(y):
        f, n = lax.axis_index("filt"), lax.axis_size("filt")
        return [lax.dynamic_slice_in_dim(y, (f + s) % n * shard, shard, 3) for s in range(n)]
    out_far, = kernel_call(far_kernel, "far", 4, sides, shape, False, (tall, far, keep, part_sum, k1, b1, k2, b2))
    out = jnp.where(odd == 1, jnp.concatenate([out_near, out_far], 0), jnp.concatenate([out_far, out_near], 0))
    return by_origin(swapped(pieces(out), "filt"), "filt", 2)


def solution(mesh):
    in_specs = (P("depth", "height", None, "filt"), P(), P(), P(), P())
    out_specs = P("depth", "height", None, "filt")
    return jax.shard_map(body, mesh=mesh, in_specs=in_specs, out_specs=out_specs, check_vma=False)
```

```python
import functools

import jax
import jax.numpy as jnp
from jax import lax
from jax.experimental import pallas as pl
from jax.experimental.pallas import tpu as pltpu
from jax.sharding import PartitionSpec as P

VMEM = pl.BlockSpec(memory_space=pltpu.VMEM)
HBM = pl.BlockSpec(memory_space=pltpu.HBM)


def leaky(value):
    return jnp.where(value > 0, value, 0.3 * value)


def pairings(peers):
    rounds = []
    for start in (0, 1):
        pairs = [(i, i + 1) for i in range(start, peers - 1, 2)]
        busy = {i for pair in pairs for i in pair}
        rounds.append(pairs + [(j, i) for i, j in pairs] + [(i, i) for i in range(peers) if i not in busy])
    return rounds


def exchange(first, last, axis):
    odd = lax.axis_index(axis) % 2 == 1
    near, far = pairings(lax.axis_size(axis))
    one = lax.ppermute(jnp.where(odd, first, last), axis, near)
    two = lax.ppermute(jnp.where(odd, last, first), axis, far)
    return one, two


def beside(one, two, axis):
    peers, index = lax.axis_size(axis), lax.axis_index(axis)
    odd = index % 2 == 1
    before = jnp.where(odd, one, two)
    after = jnp.where(odd, two, one)
    before = jnp.where(index == 0, jnp.zeros_like(before), before)
    after = jnp.where(index == peers - 1, jnp.zeros_like(after), after)
    return before, after


def by_origin(parts, axis, dim):
    peers, index = lax.axis_size(axis), lax.axis_index(axis)
    if peers == 2:
        return jnp.where(index == 0, jnp.concatenate(parts, dim), jnp.concatenate(parts[::-1], dim))
    stacked = jnp.stack(parts)
    order = (index - jnp.arange(peers)) % peers
    return jnp.concatenate([stacked[order[c]] for c in range(peers)], dim)


def swapped(pieces, axis):
    peers = lax.axis_size(axis)
    moves = [[(i, (i + s) % peers) for i in range(peers)] for s in range(peers)]
    return [pieces[0]] + [lax.ppermute(pieces[s], axis, moves[s]) for s in range(1, peers)]


def in_order(parts, axis):
    return by_origin(parts, axis, 3)


def gathered(x, columns, rows, extra):
    nc, nr = lax.axis_size(columns), lax.axis_size(rows)
    c, r = lax.axis_index(columns), lax.axis_index(rows)
    own, shard = x.shape[2] // nc, x.shape[3]
    odd = r % 2 == 1

    def window(s, x):
        block = (c + s) % nc
        if nc == 2:
            return lax.dynamic_slice_in_dim(x, block * (own - 8), own + 8, 2)
        padded = jnp.pad(x, ((0, 0), (0, 0), (2, 2), (0, 0)))
        return lax.dynamic_slice_in_dim(padded, block * own, own + 4, 2)

    def halves(s, near):
        block = (c + s) % nc
        if nc == 2:
            main = jnp.where(block == 0, near[:, :, :own], near[:, :, 8:])
            ends = jnp.where(block == 0, near[:, :, own:own + 2], near[:, :, 6:8])
        else:
            main, ends = near[:, :, 2:-2], jnp.concatenate([near[:, :, :2], near[:, :, -2:]], 2)

        def flat(rows):
            return jnp.concatenate([main[:, rows].reshape(-1, shard), ends[:, rows].reshape(-1, shard)], 0)
        first, last = flat(slice(0, 2)), flat(slice(2, 4))
        return jnp.where(odd, first, last), jnp.where(odd, last, first)

    windows = lax.optimization_barrier([window(s, x) for s in range(1, nc)])
    sent = [halves(s, windows[s - 1]) for s in range(1, nc)]
    again, extra = lax.optimization_barrier((x, extra))
    kept = halves(0, lax.optimization_barrier(window(0, again)))
    got = []
    for r_ in range(2):
        parts = [kept[r_]] + [lax.ppermute(sent[s - 1][r_], columns, [(i, (i + s) % nc) for i in range(nc)]) for s in range(1, nc)]
        got.append(by_origin(parts, columns, 1))
    near, far = pairings(nr)
    one = lax.ppermute(got[0], rows, near)
    two = lax.ppermute(got[1], rows, far)
    before, after = beside(one, two, rows)
    inner = jnp.where(odd, jnp.stack(got), jnp.stack(got[::-1]))
    return jnp.concatenate([before[None], inner, after[None]], 0), extra


def depth_rows(pairs, first, depth, own):
    ends = pairs.shape[1] // depth // 2 - own
    at = 2 * first * own, 2 * (depth * own + first * ends)
    main = pairs[:, at[0]:at[0] + 4 * own].reshape(-1, pairs.shape[2])
    return jnp.concatenate([main, pairs[:, at[1]:at[1] + 4 * ends].reshape(-1, pairs.shape[2])], 0)


def from_pairs(ref, own, depth):
    def row(d):
        pairs, C = ref.shape[0], ref.shape[2]
        ends = ref.shape[1] // depth // 2 - own
        main = [ref[p, 2 * d * own:2 * (d + 1) * own, :].reshape(2, own, C) for p in range(pairs)]
        tail = [ref[p, 2 * depth * own:, :].astype(jnp.float32)[2 * d * ends:2 * (d + 1) * ends] for p in range(pairs)]
        return jnp.concatenate(main, 0), tail
    return row


def from_rows(ref, own, pairs):
    def row(d):
        C = ref.shape[1]
        ends = ref.shape[0] // pairs // 4 - own
        main = [ref[(2 * p + d) * 2 * own:(2 * p + d + 1) * 2 * own, :].reshape(2, own, C) for p in range(pairs)]
        tail = ref[4 * pairs * own:, :].astype(jnp.float32)
        return jnp.concatenate(main, 0), [tail[(2 * p + d) * 2 * ends:(2 * p + d + 1) * 2 * ends] for p in range(pairs)]
    return row


def either(odd, one, two):
    return jax.tree.map(lambda a, b: jnp.where(odd == 1, a, b), one, two)


def spread(source, rows, at, sides, info, x3, ef, et, eb):
    H, own, C = x3.shape[1], x3.shape[2], x3.shape[3] // 3
    column = lax.broadcasted_iota(jnp.int32, (own, C), 0)
    f, none = info[4], jnp.zeros((H, C), jnp.float32)
    ends = 2 * sides
    for d in range(rows):
        x, tail = source(d)
        row = at + d
        picks = [x[:, own - 1:own, :], x[:, 0:1, :]]
        if sides == 1:
            picks = [jnp.where(f == 0, picks[0], picks[1])]
        edge = [[] for _ in range(ends + len(picks))]
        for l in range(0, C, 128):
            for p, part in enumerate(tail):
                et[l // 128, 2 * p * ends:2 * (p + 1) * ends, :] = part[:, l:l + 128]
            for e in range(ends):
                edge[e].append(et[l // 128, pl.ds(e, H, stride=ends), :])
            for k, pick in enumerate(picks):
                for h in range(H):
                    ef[k, l // 128, h * 8:h * 8 + 1, :] = pick[h, :, l:l + 128].astype(jnp.float32)
                edge[ends + k].append(ef[k, l // 128, pl.ds(0, H, stride=8), :])
        edge = [jnp.concatenate(e, 1) for e in edge]
        if sides == 1:
            e0, e1, inner = edge
            left, right = jnp.where(f == 0, none, e1), jnp.where(f == 0, e0, none)
            taps = [[jnp.where(f == 0, inner, e0), jnp.where(f == 0, e0, e1), jnp.where(f == 0, e1, inner)]]
        else:
            l0, l1, r0, r1, last, first = edge
            left, right = l1, r0
            taps = [[l0, l1, first], [last, r0, r1]]
        for s in range(sides):
            wide = jnp.concatenate(taps[s], 1)
            for b in range(3):
                moved = wide if b == 0 else pltpu.roll(wide, H - b, 0)
                eb[s, b, row] = moved.astype(jnp.bfloat16)
        for h in range(H):
            line = x[h].astype(jnp.float32)
            x3[row, h, :, 0:C] = jnp.where(column == 0, left[h:h + 1], pltpu.roll(line, 1, 0)).astype(jnp.bfloat16)
            x3[row, h, :, C:2 * C] = x[h]
            x3[row, h, :, 2 * C:] = jnp.where(column == own - 1, right[h:h + 1], pltpu.roll(line, own - 1, 0)).astype(jnp.bfloat16)


def clear(rows, at, x3, eb):
    for d in range(rows):
        x3[at + d] = jnp.zeros(x3.shape[1:], x3.dtype)
        for s in range(eb.shape[0]):
            for b in range(3):
                eb[s, b, at + d] = jnp.zeros(eb.shape[3:], eb.dtype)


def hidden_sums(d, taps, ends, x3, eb, k1, acc):
    H, own, C = x3.shape[1], x3.shape[2], x3.shape[3] // 3
    main = (H - 2) * own
    for a in taps:
        for b in range(3):
            lhs = [x3[d + a, b:b + H - 2].reshape(main, 3 * C)]
            if ends:
                lhs += [eb[s, b, a:a + ends].reshape(ends * H, 3 * C) for s in range(eb.shape[0])]
            acc += jnp.dot(jnp.concatenate(lhs, 0), k1[a, b].reshape(3 * C, C), preferred_element_type=jnp.float32)
    return acc


def hidden_rows(d, at, depth, sides, info, own, H, raw, ends, h3):
    C = raw.shape[2]
    count = ends.shape[0] // (sides * H)
    column = lax.broadcasted_iota(jnp.int32, (own, C), 0)
    none = jnp.zeros((1, C), jnp.float32)
    inside = jnp.logical_and(depth >= 0, depth < info[1])
    for h in range(H - 2):
        ok = inside
        if h == 0:
            ok = jnp.logical_and(ok, info[2] == 0)
        if h == H - 3:
            ok = jnp.logical_and(ok, info[3] == 0)
        row = jnp.where(ok, raw[d, h * own:(h + 1) * own, :], 0.0)
        edge = [ends[(s * count + d) * H + h:(s * count + d) * H + h + 1, :] for s in range(sides)]
        left = jnp.where(jnp.logical_and(ok, info[4] > 0), edge[0], none)
        right = jnp.where(jnp.logical_and(ok, info[4] < info[5] - 1), edge[sides - 1], none)
        h3[at, h, :, 0:C] = jnp.where(column == 0, left, pltpu.roll(row, 1, 0)).astype(jnp.bfloat16)
        h3[at, h, :, C:2 * C] = row.astype(jnp.bfloat16)
        h3[at, h, :, 2 * C:] = jnp.where(column == own - 1, right, pltpu.roll(row, own - 1, 0)).astype(jnp.bfloat16)


def hidden_part(d, taps, x3, eb, k1, bias, raw, ends, outer):
    main, C = raw.shape[1:]
    size = ends.shape[0] if outer else 0
    if taps[0] == 0:
        acc = jnp.zeros((main + size, C), jnp.float32)
    else:
        acc = jnp.concatenate([raw[d], ends[...]], 0) if size else raw[d]
    acc = hidden_sums(d, taps, raw.shape[0] if size else 0, x3, eb, k1, acc)
    if taps[-1] == 2:
        acc = leaky(acc + bias[...])
    raw[d] = acc[:main]
    if size:
        ends[...] = acc[main:]


def feature_sums(terms, k2, acc):
    for pair, a in terms:
        H1, own, C = pair.shape[1], pair.shape[2], pair.shape[3] // 3
        H0 = H1 - 2
        for b in range(3):
            lhs = pair[:, b:b + H0].reshape(2 * H0 * own, 3 * C)
            acc += jnp.dot(lhs, k2[a, b].reshape(3 * C, C), preferred_element_type=jnp.float32)
    return acc


def features(acc, bias, o_ref):
    o_ref[...] = leaky(acc + bias[...]).astype(jnp.bfloat16).reshape(o_ref.shape)


def places(rows):
    d, h, f = (lax.axis_index(a) for a in ("depth", "height", "filt"))
    nd, nh, nf = (lax.axis_size(a) for a in ("depth", "height", "filt"))
    odd = lax.rem(d, 2)
    end = (d == nd - 1).astype(jnp.int32)
    start = (d == 0).astype(jnp.int32)
    return (d * rows, nd * rows, (h == 0).astype(jnp.int32), (h == nh - 1).astype(jnp.int32), f, nf, odd,
            end * (1 - odd), jnp.where(odd == 1, end, start))


def near_kernel(sides, depth, xc, xn, k0, k1h, b1, k2h, b2, o_ref, keep, part_sum, k1, k2, x3, ef, et, eb, h3, raw, ends, total, sems):
    copies = [pltpu.make_async_copy(k1h.at[a], k1.at[a], sems.at[a]) for a in range(3)]
    copies += [pltpu.make_async_copy(k2h.at[a], k2.at[a], sems.at[3 + a]) for a in range(3)]
    for copy in copies[1:3]:
        copy.start()
    D, H, own = depth, x3.shape[1], x3.shape[2]
    info = places(D)
    odd = info[6]
    scratch = (x3, ef, et, eb)
    tall, near = from_pairs(xc, own, D), from_rows(xn, own, H // 2)

    def lay(r):
        def source(_):
            if r < 2:
                return either(odd, near(r), tall(r))
            return either(odd, tall(r - 2), tall(r) if r < D else near(r - D))
        spread(source, 1, r, sides, info, *scratch)

    first = info[0] - 1 + 2 * (1 - odd)

    def block(run):
        pl.when(odd >= 0)(run)

    def part(d, taps):
        hidden_part(d, taps, x3, eb, k1 if taps[0] else k0, b1, raw, ends, d == (0 if taps[0] else D - 1))

    def rows(d):
        hidden_rows(d, d, first + d, sides, info, own, H, raw, ends, h3)

    for a in range(3):
        if a > 0:
            copies[a].wait()
        if a == 1:
            for copy in copies[3:] + copies[:1]:
                copy.start()

        @block
        def _():
            for d in range(D):
                if a == 0:
                    lay(d)
                part(d, [a])
                if a == 2:
                    rows(d)
            if a == 0:
                lay(D)
                lay(D + 1)

        if a == 0:
            @pl.when(info[7] > 0)
            def _():
                clear(2, D, x3, eb)
    for copy in copies[3:] + copies[:1]:
        copy.wait()

    @block
    def _():
        keep[...] = h3[pl.ds((D - 2) * odd, 2)]
        part_sum[...] = feature_sums([(h3.at[pl.ds((D - 2) * odd, 2)], 2 * (1 - odd))], k2, jnp.zeros(part_sum.shape, jnp.float32))
        features(feature_sums([(h3.at[a:a + 2], a) for a in range(3)], k2, jnp.zeros(total.shape, jnp.float32)), b2, o_ref)


def far_kernel(sides, depth, xc, xf, keep, part_sum, k1, b1, k2, b2, o_ref, x3, ef, et, eb, h3, raw, ends, total):
    D, H, own = depth, x3.shape[1], x3.shape[2]
    info = places(D)
    odd = info[6]
    scratch = (x3, ef, et, eb)
    tall = from_pairs(xc, own, D)
    first = info[0] - 1 + D * odd
    known = 2 * (1 - odd)

    @pl.when(odd >= 0)
    def _():
        spread(lambda d: either(odd, tall(D - 2 + d), tall(d)), 2, 2 * (1 - odd), sides, info, *scratch)
        spread(from_rows(xf, own, H // 2), 2, 2 * odd, sides, info, *scratch)
        h3[pl.ds(known, 2)] = keep[...]

    @pl.when(info[8] > 0)
    def _():
        clear(2, 2 * odd, x3, eb)

    @pl.when(odd >= 0)
    def _():
        for d in range(2):
            hidden_part(d, range(3), x3, eb, k1, b1, raw, ends, d == 0)
        for d in range(2):
            hidden_rows(d, 2 * odd + d, first + d, sides, info, own, H, raw, ends, h3)

    @pl.when(odd >= 0)
    def _():
        features(feature_sums([(h3.at[1:3], 1), (h3.at[pl.ds(2 * odd, 2)], 2 * odd)], k2, part_sum[...]), b2, o_ref)


def kernel_call(kernel, name, rows, sides, shape, near, operands):
    D, H, own, C = shape
    weights = jax.ShapeDtypeStruct((3, 3, 3, C, C), jnp.bfloat16)
    out = [jax.ShapeDtypeStruct((2, H - 4, own, C), jnp.bfloat16)]
    scratch = [
        pltpu.VMEM((rows, H, own, 3 * C), jnp.bfloat16),
        pltpu.VMEM((sides, C // 128, H * 8, 128), jnp.float32),
        pltpu.VMEM((C // 128, 2 * sides * H, 128), jnp.float32),
        pltpu.VMEM((sides, 3, rows, H, 3 * C), jnp.bfloat16),
        pltpu.VMEM((4, H - 2, own, 3 * C), jnp.bfloat16),
        pltpu.VMEM((rows - 2, (H - 2) * own, C), jnp.float32),
        pltpu.VMEM((sides * (rows - 2) * H, C), jnp.float32),
        pltpu.VMEM((2 * (H - 4) * own, C), jnp.float32),
    ]
    specs = [VMEM] * len(operands)
    if near:
        out += [jax.ShapeDtypeStruct((2, H - 2, own, 3 * C), jnp.bfloat16), jax.ShapeDtypeStruct((2 * (H - 4) * own, C), jnp.float32), weights, weights]
        scratch.append(pltpu.SemaphoreType.DMA((6,)))
        specs[3] = specs[5] = HBM
    hid = (rows - 2) * (H - 2) * own
    return pl.pallas_call(
        functools.partial(kernel, sides, D),
        out_shape=out,
        in_specs=specs,
        out_specs=[VMEM] * len(out),
        scratch_shapes=scratch,
        compiler_params=pltpu.CompilerParams(vmem_limit_bytes=(43 if near else 24) * 2**20),
        cost_estimate=pl.CostEstimate(flops=2 * 27 * C * C * (hid + 2 * (H - 4) * own), bytes_accessed=2**20, transcendentals=0),
        name=name,
    )(*operands)


def body(volume, kernel_one, bias_one, kernel_two, bias_two):
    b1, b2 = bias_one.reshape(1, -1), bias_two.reshape(1, -1)
    rows, odd = volume.shape[0], lax.axis_index("depth") % 2
    sides = 1 if lax.axis_size("filt") == 2 else 2

    tall, k0 = gathered(volume, "filt", "height", kernel_one[:1])
    own, wide = volume.shape[2] // lax.axis_size("filt"), bias_one.shape[0]
    shape = (rows, volume.shape[1] + 4, own, wide)
    near, far = exchange(depth_rows(tall, 0, rows, own), depth_rows(tall, rows - 2, rows, own), "depth")
    out_near, keep, part_sum, k1, k2 = kernel_call(near_kernel, "near", rows + 2, sides, shape, True, (tall, near, k0, kernel_one, b1, kernel_two, b2))
    shard = volume.shape[3]
    def pieces(y):
        f, n = lax.axis_index("filt"), lax.axis_size("filt")
        return [lax.dynamic_slice_in_dim(y, (f + s) % n * shard, shard, 3) for s in range(n)]
    out_far, = kernel_call(far_kernel, "far", 4, sides, shape, False, (tall, far, keep, part_sum, k1, b1, k2, b2))
    out = jnp.where(odd == 1, jnp.concatenate([out_near, out_far], 0), jnp.concatenate([out_far, out_near], 0))
    return by_origin(swapped(pieces(out), "filt"), "filt", 2)


def solution(mesh):
    in_specs = (P("depth", "height", None, "filt"), P(), P(), P(), P())
    out_specs = P("depth", "height", None, "filt")
    return jax.shard_map(body, mesh=mesh, in_specs=in_specs, out_specs=out_specs, check_vma=False)
```

```python
import functools

import jax
import jax.numpy as jnp
from jax import lax
from jax.experimental import pallas as pl
from jax.experimental.pallas import tpu as pltpu
from jax.sharding import PartitionSpec as P

VMEM = pl.BlockSpec(memory_space=pltpu.VMEM)
HBM = pl.BlockSpec(memory_space=pltpu.HBM)


def leaky(value):
    return jnp.where(value > 0, value, 0.3 * value)


def pairings(peers):
    rounds = []
    for start in (0, 1):
        pairs = [(i, i + 1) for i in range(start, peers - 1, 2)]
        busy = {i for pair in pairs for i in pair}
        rounds.append(pairs + [(j, i) for i, j in pairs] + [(i, i) for i in range(peers) if i not in busy])
    return rounds


def exchange(first, last, axis):
    odd = lax.axis_index(axis) % 2 == 1
    near, far = pairings(lax.axis_size(axis))
    one = lax.ppermute(jnp.where(odd, first, last), axis, near)
    two = lax.ppermute(jnp.where(odd, last, first), axis, far)
    return one, two


def beside(one, two, axis):
    peers, index = lax.axis_size(axis), lax.axis_index(axis)
    odd = index % 2 == 1
    before = jnp.where(odd, one, two)
    after = jnp.where(odd, two, one)
    before = jnp.where(index == 0, jnp.zeros_like(before), before)
    after = jnp.where(index == peers - 1, jnp.zeros_like(after), after)
    return before, after


def by_origin(parts, axis, dim):
    peers, index = lax.axis_size(axis), lax.axis_index(axis)
    if peers == 2:
        return jnp.where(index == 0, jnp.concatenate(parts, dim), jnp.concatenate(parts[::-1], dim))
    stacked = jnp.stack(parts)
    order = (index - jnp.arange(peers)) % peers
    return jnp.concatenate([stacked[order[c]] for c in range(peers)], dim)


def swapped(pieces, axis):
    peers = lax.axis_size(axis)
    moves = [[(i, (i + s) % peers) for i in range(peers)] for s in range(peers)]
    return [pieces[0]] + [lax.ppermute(pieces[s], axis, moves[s]) for s in range(1, peers)]


def in_order(parts, axis):
    return by_origin(parts, axis, 3)


def gathered(x, columns, rows, extra):
    nc, nr = lax.axis_size(columns), lax.axis_size(rows)
    c, r = lax.axis_index(columns), lax.axis_index(rows)
    own, shard = x.shape[2] // nc, x.shape[3]
    odd = r % 2 == 1

    def window(s, x):
        block = (c + s) % nc
        if nc == 2:
            return lax.dynamic_slice_in_dim(x, block * (own - 8), own + 8, 2)
        padded = jnp.pad(x, ((0, 0), (0, 0), (2, 2), (0, 0)))
        return lax.dynamic_slice_in_dim(padded, block * own, own + 4, 2)

    def halves(s, near):
        block = (c + s) % nc
        if nc == 2:
            main = jnp.where(block == 0, near[:, :, :own], near[:, :, 8:])
            ends = jnp.where(block == 0, near[:, :, own:own + 2], near[:, :, 6:8])
        else:
            main, ends = near[:, :, 2:-2], jnp.concatenate([near[:, :, :2], near[:, :, -2:]], 2)

        def flat(rows):
            return jnp.concatenate([main[:, rows].reshape(-1, shard), ends[:, rows].reshape(-1, shard)], 0)
        first, last = flat(slice(0, 2)), flat(slice(2, 4))
        return jnp.where(odd, first, last), jnp.where(odd, last, first)

    windows = lax.optimization_barrier([window(s, x) for s in range(1, nc)])
    sent = [halves(s, windows[s - 1]) for s in range(1, nc)]
    again, extra = lax.optimization_barrier((x, extra))
    kept = halves(0, lax.optimization_barrier(window(0, again)))
    got = []
    for r_ in range(2):
        parts = [kept[r_]] + [lax.ppermute(sent[s - 1][r_], columns, [(i, (i + s) % nc) for i in range(nc)]) for s in range(1, nc)]
        got.append(by_origin(parts, columns, 1))
    near, far = pairings(nr)
    one = lax.ppermute(got[0], rows, near)
    two = lax.ppermute(got[1], rows, far)
    before, after = beside(one, two, rows)
    inner = jnp.where(odd, jnp.stack(got), jnp.stack(got[::-1]))
    return jnp.concatenate([before[None], inner, after[None]], 0), extra


def depth_rows(pairs, first, depth, own):
    ends = pairs.shape[1] // depth // 2 - own
    at = 2 * first * own, 2 * (depth * own + first * ends)
    main = pairs[:, at[0]:at[0] + 4 * own].reshape(-1, pairs.shape[2])
    return jnp.concatenate([main, pairs[:, at[1]:at[1] + 4 * ends].reshape(-1, pairs.shape[2])], 0)


def from_pairs(ref, own, depth):
    def row(d):
        pairs, C = ref.shape[0], ref.shape[2]
        ends = ref.shape[1] // depth // 2 - own
        main = [ref[p, 2 * d * own:2 * (d + 1) * own, :].reshape(2, own, C) for p in range(pairs)]
        tail = [ref[p, 2 * depth * own:, :].astype(jnp.float32)[2 * d * ends:2 * (d + 1) * ends] for p in range(pairs)]
        return jnp.concatenate(main, 0), tail
    return row


def from_rows(ref, own, pairs):
    def row(d):
        C = ref.shape[1]
        ends = ref.shape[0] // pairs // 4 - own
        main = [ref[(2 * p + d) * 2 * own:(2 * p + d + 1) * 2 * own, :].reshape(2, own, C) for p in range(pairs)]
        tail = ref[4 * pairs * own:, :].astype(jnp.float32)
        return jnp.concatenate(main, 0), [tail[(2 * p + d) * 2 * ends:(2 * p + d + 1) * 2 * ends] for p in range(pairs)]
    return row


def either(odd, one, two):
    return jax.tree.map(lambda a, b: jnp.where(odd == 1, a, b), one, two)


def spread(source, rows, at, sides, info, x3, ef, et, eb):
    H, own, C = x3.shape[1], x3.shape[2], x3.shape[3] // 3
    column = lax.broadcasted_iota(jnp.int32, (own, C), 0)
    f, none = info[4], jnp.zeros((H, C), jnp.float32)
    ends = 2 * sides
    for d in range(rows):
        x, tail = source(d)
        row = at + d
        picks = [x[:, own - 1:own, :], x[:, 0:1, :]]
        if sides == 1:
            picks = [jnp.where(f == 0, picks[0], picks[1])]
        edge = [[] for _ in range(ends + len(picks))]
        for l in range(0, C, 128):
            for p, part in enumerate(tail):
                et[l // 128, 2 * p * ends:2 * (p + 1) * ends, :] = part[:, l:l + 128]
            for e in range(ends):
                edge[e].append(et[l // 128, pl.ds(e, H, stride=ends), :])
            for k, pick in enumerate(picks):
                for h in range(H):
                    ef[k, l // 128, h * 8:h * 8 + 1, :] = pick[h, :, l:l + 128].astype(jnp.float32)
                edge[ends + k].append(ef[k, l // 128, pl.ds(0, H, stride=8), :])
        edge = [jnp.concatenate(e, 1) for e in edge]
        if sides == 1:
            e0, e1, inner = edge
            left, right = jnp.where(f == 0, none, e1), jnp.where(f == 0, e0, none)
            taps = [[jnp.where(f == 0, inner, e0), jnp.where(f == 0, e0, e1), jnp.where(f == 0, e1, inner)]]
        else:
            l0, l1, r0, r1, last, first = edge
            left, right = l1, r0
            taps = [[l0, l1, first], [last, r0, r1]]
        for s in range(sides):
            wide = jnp.concatenate(taps[s], 1)
            for b in range(3):
                moved = wide if b == 0 else pltpu.roll(wide, H - b, 0)
                eb[s, b, row] = moved.astype(jnp.bfloat16)
        for h in range(H):
            line = x[h].astype(jnp.float32)
            x3[row, h, :, 0:C] = jnp.where(column == 0, left[h:h + 1], pltpu.roll(line, 1, 0)).astype(jnp.bfloat16)
            x3[row, h, :, C:2 * C] = x[h]
            x3[row, h, :, 2 * C:] = jnp.where(column == own - 1, right[h:h + 1], pltpu.roll(line, own - 1, 0)).astype(jnp.bfloat16)


def clear(rows, at, x3, eb):
    for d in range(rows):
        x3[at + d] = jnp.zeros(x3.shape[1:], x3.dtype)
        for s in range(eb.shape[0]):
            for b in range(3):
                eb[s, b, at + d] = jnp.zeros(eb.shape[3:], eb.dtype)


def hidden_sums(d, taps, ends, x3, eb, k1, acc):
    H, own, C = x3.shape[1], x3.shape[2], x3.shape[3] // 3
    main = (H - 2) * own
    for a in taps:
        for b in range(3):
            lhs = [x3[d + a, b:b + H - 2].reshape(main, 3 * C)]
            if ends:
                lhs += [eb[s, b, a:a + ends].reshape(ends * H, 3 * C) for s in range(eb.shape[0])]
            acc += jnp.dot(jnp.concatenate(lhs, 0), k1[a, b].reshape(3 * C, C), preferred_element_type=jnp.float32)
    return acc


def hidden_rows(d, at, depth, sides, info, own, H, raw, ends, h3):
    C = raw.shape[2]
    count = ends.shape[0] // (sides * H)
    column = lax.broadcasted_iota(jnp.int32, (own, C), 0)
    none = jnp.zeros((1, C), jnp.float32)
    inside = jnp.logical_and(depth >= 0, depth < info[1])
    for h in range(H - 2):
        ok = inside
        if h == 0:
            ok = jnp.logical_and(ok, info[2] == 0)
        if h == H - 3:
            ok = jnp.logical_and(ok, info[3] == 0)
        row = jnp.where(ok, raw[d, h * own:(h + 1) * own, :], 0.0)
        edge = [ends[(s * count + d) * H + h:(s * count + d) * H + h + 1, :] for s in range(sides)]
        left = jnp.where(jnp.logical_and(ok, info[4] > 0), edge[0], none)
        right = jnp.where(jnp.logical_and(ok, info[4] < info[5] - 1), edge[sides - 1], none)
        h3[at, h, :, 0:C] = jnp.where(column == 0, left, pltpu.roll(row, 1, 0)).astype(jnp.bfloat16)
        h3[at, h, :, C:2 * C] = row.astype(jnp.bfloat16)
        h3[at, h, :, 2 * C:] = jnp.where(column == own - 1, right, pltpu.roll(row, own - 1, 0)).astype(jnp.bfloat16)


def hidden_part(d, taps, x3, eb, k1, bias, raw, ends, outer):
    main, C = raw.shape[1:]
    size = ends.shape[0] if outer else 0
    if taps[0] == 0:
        acc = jnp.zeros((main + size, C), jnp.float32)
    else:
        acc = jnp.concatenate([raw[d], ends[...]], 0) if size else raw[d]
    acc = hidden_sums(d, taps, raw.shape[0] if size else 0, x3, eb, k1, acc)
    if taps[-1] == 2:
        acc = leaky(acc + bias[...])
    raw[d] = acc[:main]
    if size:
        ends[...] = acc[main:]


def feature_sums(terms, k2, acc):
    for pair, a in terms:
        H1, own, C = pair.shape[1], pair.shape[2], pair.shape[3] // 3
        H0 = H1 - 2
        for b in range(3):
            lhs = pair[:, b:b + H0].reshape(2 * H0 * own, 3 * C)
            acc += jnp.dot(lhs, k2[a, b].reshape(3 * C, C), preferred_element_type=jnp.float32)
    return acc


def features(acc, bias, o_ref):
    o_ref[...] = leaky(acc + bias[...]).astype(jnp.bfloat16).reshape(o_ref.shape)


def places(rows):
    d, h, f = (lax.axis_index(a) for a in ("depth", "height", "filt"))
    nd, nh, nf = (lax.axis_size(a) for a in ("depth", "height", "filt"))
    odd = lax.rem(d, 2)
    end = (d == nd - 1).astype(jnp.int32)
    start = (d == 0).astype(jnp.int32)
    return (d * rows, nd * rows, (h == 0).astype(jnp.int32), (h == nh - 1).astype(jnp.int32), f, nf, odd,
            end * (1 - odd), jnp.where(odd == 1, end, start))


def near_kernel(sides, depth, xc, xn, k0, k1h, b1, k2h, b2, o_ref, keep, part_sum, k1, k2, x3, ef, et, eb, h3, raw, ends, total, sems):
    copies = [pltpu.make_async_copy(k1h.at[a], k1.at[a], sems.at[a]) for a in range(3)]
    copies += [pltpu.make_async_copy(k2h.at[a], k2.at[a], sems.at[3 + a]) for a in range(3)]
    for copy in copies[1:3]:
        copy.start()
    D, H, own = depth, x3.shape[1], x3.shape[2]
    info = places(D)
    odd = info[6]
    scratch = (x3, ef, et, eb)
    tall, near = from_pairs(xc, own, D), from_rows(xn, own, H // 2)

    def lay(r):
        def source(_):
            if r < 2:
                return either(odd, near(r), tall(r))
            return either(odd, tall(r - 2), tall(r) if r < D else near(r - D))
        spread(source, 1, r, sides, info, *scratch)

    first = info[0] - 1 + 2 * (1 - odd)

    def block(run):
        pl.when(odd >= 0)(run)

    def part(d, taps):
        hidden_part(d, taps, x3, eb, k1 if taps[0] else k0, b1, raw, ends, d == (0 if taps[0] else D - 1))

    def rows(d):
        hidden_rows(d, d, first + d, sides, info, own, H, raw, ends, h3)

    for a in range(3):
        if a > 0:
            copies[a].wait()
        if a == 1:
            for copy in copies[3:] + copies[:1]:
                copy.start()

        @block
        def _():
            for d in range(D):
                if a == 0:
                    lay(d)
                part(d, [a])
                if a == 2:
                    rows(d)
            if a == 0:
                lay(D)
                lay(D + 1)

        if a == 0:
            @pl.when(info[7] > 0)
            def _():
                clear(2, D, x3, eb)
    for copy in copies[3:] + copies[:1]:
        copy.wait()

    @block
    def _():
        keep[...] = h3[pl.ds((D - 2) * odd, 2)]
        part_sum[...] = feature_sums([(h3.at[pl.ds((D - 2) * odd, 2)], 2 * (1 - odd))], k2, jnp.zeros(part_sum.shape, jnp.float32))
        features(feature_sums([(h3.at[a:a + 2], a) for a in range(3)], k2, jnp.zeros(total.shape, jnp.float32)), b2, o_ref)


def far_kernel(sides, depth, xc, xf, keep, part_sum, k1, b1, k2, b2, o_ref, x3, ef, et, eb, h3, raw, ends, total):
    D, H, own = depth, x3.shape[1], x3.shape[2]
    info = places(D)
    odd = info[6]
    scratch = (x3, ef, et, eb)
    tall = from_pairs(xc, own, D)
    first = info[0] - 1 + D * odd
    known = 2 * (1 - odd)

    @pl.when(odd >= 0)
    def _():
        spread(lambda d: either(odd, tall(D - 2 + d), tall(d)), 2, 2 * (1 - odd), sides, info, *scratch)
        spread(from_rows(xf, own, H // 2), 2, 2 * odd, sides, info, *scratch)
        h3[pl.ds(known, 2)] = keep[...]

    @pl.when(info[8] > 0)
    def _():
        clear(2, 2 * odd, x3, eb)

    @pl.when(odd >= 0)
    def _():
        for d in range(2):
            hidden_part(d, range(3), x3, eb, k1, b1, raw, ends, d == 0)
        for d in range(2):
            hidden_rows(d, 2 * odd + d, first + d, sides, info, own, H, raw, ends, h3)

    @pl.when(odd >= 0)
    def _():
        features(feature_sums([(h3.at[1:3], 1), (h3.at[pl.ds(2 * odd, 2)], 2 * odd)], k2, part_sum[...]), b2, o_ref)


def kernel_call(kernel, name, rows, sides, shape, near, operands):
    D, H, own, C = shape
    weights = jax.ShapeDtypeStruct((3, 3, 3, C, C), jnp.bfloat16)
    out = [jax.ShapeDtypeStruct((2, H - 4, own, C), jnp.bfloat16)]
    scratch = [
        pltpu.VMEM((rows, H, own, 3 * C), jnp.bfloat16),
        pltpu.VMEM((sides, C // 128, H * 8, 128), jnp.float32),
        pltpu.VMEM((C // 128, 2 * sides * H, 128), jnp.float32),
        pltpu.VMEM((sides, 3, rows, H, 3 * C), jnp.bfloat16),
        pltpu.VMEM((4, H - 2, own, 3 * C), jnp.bfloat16),
        pltpu.VMEM((rows - 2, (H - 2) * own, C), jnp.float32),
        pltpu.VMEM((sides * (rows - 2) * H, C), jnp.float32),
        pltpu.VMEM((2 * (H - 4) * own, C), jnp.float32),
    ]
    specs = [VMEM] * len(operands)
    if near:
        out += [jax.ShapeDtypeStruct((2, H - 2, own, 3 * C), jnp.bfloat16), jax.ShapeDtypeStruct((2 * (H - 4) * own, C), jnp.float32), weights, weights]
        scratch.append(pltpu.SemaphoreType.DMA((6,)))
        specs[3] = specs[5] = HBM
    hid = (rows - 2) * (H - 2) * own
    return pl.pallas_call(
        functools.partial(kernel, sides, D),
        out_shape=out,
        in_specs=specs,
        out_specs=[VMEM] * len(out),
        scratch_shapes=scratch,
        compiler_params=pltpu.CompilerParams(vmem_limit_bytes=(43 if near else 24) * 2**20),
        cost_estimate=pl.CostEstimate(flops=2 * 27 * C * C * (hid + 2 * (H - 4) * own), bytes_accessed=2**20, transcendentals=0),
        name=name,
    )(*operands)


def body(volume, kernel_one, bias_one, kernel_two, bias_two):
    b1, b2 = bias_one.reshape(1, -1), bias_two.reshape(1, -1)
    rows, odd = volume.shape[0], lax.axis_index("depth") % 2
    sides = 1 if lax.axis_size("filt") == 2 else 2

    tall, k0 = gathered(volume, "filt", "height", kernel_one[:1])
    own, wide = volume.shape[2] // lax.axis_size("filt"), bias_one.shape[0]
    shape = (rows, volume.shape[1] + 4, own, wide)
    near, far = exchange(depth_rows(tall, 0, rows, own), depth_rows(tall, rows - 2, rows, own), "depth")
    out_near, keep, part_sum, k1, k2 = kernel_call(near_kernel, "near", rows + 2, sides, shape, True, (tall, near, k0, kernel_one, b1, kernel_two, b2))
    shard = volume.shape[3]
    def pieces(y):
        f, n = lax.axis_index("filt"), lax.axis_size("filt")
        return [lax.dynamic_slice_in_dim(y, (f + s) % n * shard, shard, 3) for s in range(n)]
    out_far, = kernel_call(far_kernel, "far", 4, sides, shape, False, (tall, far, keep, part_sum, k1, b1, k2, b2))
    out = jnp.where(odd == 1, jnp.concatenate([out_near, out_far], 0), jnp.concatenate([out_far, out_near], 0))
    parts = swapped(pieces(out), "filt")
    f, n = lax.axis_index("filt"), lax.axis_size("filt")
    result = jnp.zeros(volume.shape, volume.dtype)
    for s, part in enumerate(parts):
        result = lax.dynamic_update_slice_in_dim(result, part, (f - s) % n * own, 2)
    return result


def solution(mesh):
    in_specs = (P("depth", "height", None, "filt"), P(), P(), P(), P())
    out_specs = P("depth", "height", None, "filt")
    return jax.shard_map(body, mesh=mesh, in_specs=in_specs, out_specs=out_specs, check_vma=False)
```
